512 devices in a mesh: dp: 128 (over y, z_lo, x, core), qsplit: 4 (over z_hi).
Axes of the slice: x: 4, y: 4, z: 16 (z_hi: 4, z_lo: 4; z = z_hi * 4 + z_lo), core: 2. Of those that a mesh axis runs over, the one named last changes fastest.
Arguments:
- scores: float32 [131072], P(('dp', 'qsplit')), may hold values from -6 to 6
- grades: int32 [131072], P(('dp', 'qsplit')), may hold values from 0 to 4
- lengths: int32 [128, 128], P('dp'), may hold values from 0 to 512, as said below
- bin_codes: int32 [700, 131072], P(None, ('dp', 'qsplit')), may hold values from 0 to 255
- node_ids: int32 [131072], P(('dp', 'qsplit')), may hold values from 0 to 1
Outputs:
- grad_rows: float32 [131072], P(('dp', 'qsplit'))
- hess_rows: float32 [131072], P(('dp', 'qsplit'))
- grad_hist: float32 [2, 179200], P(None, ('dp', 'qsplit'))
- hess_hist: float32 [2, 179200], P(None, ('dp', 'qsplit'))
The draws below stay inside these ranges and needn't reach their ends.
Inputs may be any that keep to these rules, and one draw needn't show every extreme that they name: `lengths`: each row sums to 1024; every nonzero length is a multiple of 8; zeros only follow the last query of a row; every row holds one query of exactly 512 documents.
All inputs are finite; a program needn't handle non-finite values.
Results may differ from the reference program's by a relative error of at most 0.0003.
Values sent between devices are 32-bit elements; how exact they have to be, the bound alone decides.
A program may use at most 64 MiB of HBM per device.

```python
import math
import jax
import jax.numpy as jnp
from jax import lax

F = 700
BINS = 256
NODES = 2
PAIR_TILE = 128
QUNIT = 8
GROUP = 1024
L_MAX = 512
SLOTS = 128
TOTAL_ROWS = 131072
ROWS_PER_BIN = 256
N_DP = 128


def draw_lengths(key, part):
    key = jax.random.fold_in(key, 7)
    units_max = L_MAX // QUNIT
    total_units = GROUP // QUNIT
    level_count = max(int(units_max).bit_length(), 1)
    key_power, key_long = jax.random.split(key)
    powers = jax.random.randint(key_power, (N_DP, SLOTS), 0, level_count)
    unit_count = jnp.minimum(jnp.left_shift(jnp.ones_like(powers), powers), units_max)
    chosen = jax.random.randint(key_long, (N_DP, 1), 0, 2)
    slot_index = jnp.arange(SLOTS, dtype=jnp.int32)[None, :]
    unit_count = jnp.where(slot_index == chosen, units_max, unit_count)
    slot_ends = jnp.cumsum(unit_count, axis=1)
    slot_starts = slot_ends - unit_count
    kept_units = jnp.clip(total_units - slot_starts, 0, unit_count)
    return (kept_units * QUNIT).astype(jnp.int32)


def with_ends(array, own_key, smallest, top_value):
    longest = array.shape.index(max(array.shape))
    spots = []
    for shift in (0, 1):
        where = [jax.random.randint(jax.random.fold_in(own_key, axis), (), 0, length) for axis, length in enumerate(array.shape)]
        where[longest] = (where[longest] + shift) % array.shape[longest]
        spots.append(tuple(where))
    return array.at[spots[0]].set(smallest).at[spots[1]].set(top_value)


def block_scale(rng, shape, shards, smallest, high):
    gain, own = 1.0, jax.random.fold_in(rng, 6)
    for position, parts in shards:
        steps = jnp.exp(jax.random.uniform(jax.random.fold_in(own, position), (parts,), jnp.float32, smallest / len(shards), high / len(shards)))
        gain = gain * jnp.repeat(steps, shape[position] // parts).reshape([-1 if axis == position else 1 for axis in range(len(shape))])
    return gain


def scatter_about(rng, dims, scale, reach, pieces=(), kind=jnp.bfloat16):
    array = jax.random.normal(rng, dims, jnp.float32) * scale
    if len(pieces) > 0:
        array = block_scale(rng, dims, pieces, -0.22, 0.18) * array
    return jnp.clip(array, min=-reach, max=reach).astype(kind)


def setup_inputs(seed: int = 0) -> dict:
    seeds = jax.random.split(jax.random.key(seed), 6)
    return {
        "scores": scatter_about(seeds[0], (TOTAL_ROWS,), 1.0, 6.0, ((0, 512),), jnp.float32),
        "grades": with_ends(jax.random.randint(seeds[1], (TOTAL_ROWS,), 0, 5), jax.random.fold_in(seeds[1], 1), 0, 4).astype(jnp.int32),
        "lengths": draw_lengths(jax.random.fold_in(seeds[5], 71), 0),
        "bin_codes": with_ends(jax.random.randint(seeds[3], (F, TOTAL_ROWS), 0, BINS), jax.random.fold_in(seeds[3], 1), 0, BINS - 1).astype(jnp.int32),
        "node_ids": with_ends(jax.random.randint(seeds[4], (TOTAL_ROWS,), 0, NODES), jax.random.fold_in(seeds[4], 1), 0, NODES - 1).astype(jnp.int32),
    }


steepness = 1.0

def query_layout(length_row, group_rows):
    slot_ends = jnp.cumsum(length_row).astype(jnp.int32)
    slot_starts = (slot_ends - length_row).astype(jnp.int32)
    positions = jnp.arange(group_rows, dtype=jnp.int32)
    query_ids = jnp.searchsorted(slot_ends, positions, side='right').astype(jnp.int32)
    first_row = slot_starts[query_ids]
    last_end = slot_ends[query_ids]
    rank_pos = (positions - first_row).astype(jnp.float32)
    discount = 1.0 / jnp.log2(rank_pos + 2.0)
    return (query_ids, discount, first_row, last_end)

def pair_terms(own_score, own_gain, own_disc, own_query, far_score, far_gain, far_disc, far_query):
    spread = own_score[:, None] - far_score[None, :]
    gain_gap = own_gain[:, None] - far_gain[None, :]
    disc_gap = jnp.abs(own_disc[:, None] - far_disc[None, :])
    weight = jnp.where(own_query[:, None] == far_query[None, :], jnp.abs(gain_gap) * disc_gap, 0.0)
    direction = jnp.sign(gain_gap)
    pushed = weight * jax.nn.sigmoid(-direction * steepness * spread)
    curvature = weight * jax.nn.sigmoid(steepness * spread) * jax.nn.sigmoid(-steepness * spread)
    return (lax.optimization_barrier(jnp.sum(-direction * pushed, axis=1)), lax.optimization_barrier(jnp.sum(pushed, axis=1)), lax.optimization_barrier(jnp.sum(curvature, axis=1)))

def reference(scores, grades, lengths, bin_codes, node_ids):
    group_rows = GROUP

    def one_group(inputs):
        group_scores, group_grades, length_row = inputs
        query_ids, discount, first_row, last_end = query_layout(length_row, group_rows)
        gain_rows = jnp.exp2(group_grades.astype(jnp.float32)) - 1.0

        def one_block(block_start):
            own_score = lax.dynamic_slice_in_dim(group_scores, block_start, PAIR_TILE)
            own_gain = lax.dynamic_slice_in_dim(gain_rows, block_start, PAIR_TILE)
            own_disc = lax.dynamic_slice_in_dim(discount, block_start, PAIR_TILE)
            own_query = lax.dynamic_slice_in_dim(query_ids, block_start, PAIR_TILE)
            return pair_terms(own_score, own_gain, own_disc, own_query, group_scores, gain_rows, discount, query_ids)
        block_starts = jnp.arange(group_rows // PAIR_TILE, dtype=jnp.int32) * PAIR_TILE
        slope_sum, push_sum, curv_sum = lax.map(one_block, block_starts)
        slope_sum = slope_sum.reshape(-1)
        push_sum = push_sum.reshape(-1)
        curv_sum = curv_sum.reshape(-1)
        totals = jax.ops.segment_sum(push_sum, query_ids, num_segments=SLOTS)
        factor = jnp.log2(1.0 + totals) / jnp.maximum(totals, 1.0)
        row_factor = factor[query_ids]
        return (slope_sum * row_factor, curv_sum * row_factor)
    grad_rows, hess_rows = lax.map(one_group, (scores.reshape(N_DP, group_rows), grades.reshape(N_DP, group_rows), lengths))
    grad_rows = grad_rows.reshape(-1)
    hess_rows = hess_rows.reshape(-1)
    row_stats = jnp.stack([grad_rows, hess_rows], axis=1)

    def one_feature(codes):
        return jax.ops.segment_sum(row_stats, node_ids * BINS + codes, num_segments=NODES * BINS)
    per_feature = lax.map(one_feature, bin_codes).reshape(F, NODES, BINS, 2)
    hist_all = jnp.transpose(per_feature, (3, 1, 0, 2)).reshape(2, NODES, F * BINS)
    hist_all = hist_all / math.sqrt(ROWS_PER_BIN)
    return (grad_rows, hess_rows, hist_all[0], hist_all[1])
```

```python
import jax
import jax.numpy as jnp
from jax import lax
from jax.experimental import pallas as pl
from jax.experimental.pallas import tpu as pltpu
from jax.sharding import PartitionSpec as P

F32, I32, BF16 = jnp.float32, jnp.int32, jnp.bfloat16
MESH = pl.DeviceIdType.MESH

FEATURES = 700
BINS = 256
PLANE = 32
DEPTH = 16
SPLIT = 4
TILES = 8
REACH = 4
SLOTS = 24
CHUNKS = 3
PER = SLOTS // CHUNKS
QUAD = 4
LOW = BINS // QUAD
WINDOW = 3
OWNED = FEATURES * BINS // (PLANE * DEPTH)
STEP = 8
LOG2E = 1.4426950408889634


def pieces(x):
    high = x.astype(BF16)
    rest = x - high.astype(F32)
    middle = rest.astype(BF16)
    return high, middle, (rest - middle.astype(F32)).astype(BF16)


def over_rows(x):
    return jnp.sum(x.reshape(x.shape[0] // 8, 8, x.shape[1]), axis=0)


def wait_bytes(ref, sem):
    pltpu.make_async_copy(ref, ref, sem).wait()


def kernel(
    score_ref, grade_ref, length_ref, codes_hbm, node_ref,
    grad_ref, hess_ref, grad_hist_ref, hess_hist_ref,
    codes_in, codes_tx, codes_rx, pack_tx, pack_rx, stat_tx, stat_rx, split,
    query, discount, score_all, gain_all, col_fixed, col_sent, same, hist, window_rx,
    load_sem, pack_send, pack_recv, code_send, code_recv, stat_send, stat_recv, final_send, final_recv,
):
    dp, part = lax.axis_index("dp"), lax.axis_index("qsplit")
    y, z_low, inner = dp // 32, (dp // 8) % 4, dp % 8
    me = y * 8 + inner
    level = z_low * 4 + part
    block, place = dp // 4, (dp % 4) * 4 + part

    def plane_peer(other):
        return ((other // 8) * 32 + z_low * 8 + other % 8, part)

    load = pltpu.make_async_copy(codes_hbm, codes_in, load_sem)
    load.start()

    barrier = pltpu.get_barrier_semaphore()

    def greet_plane(r, carry):
        pl.semaphore_signal(barrier, inc=1, device_id=plane_peer((me + r) % PLANE), device_id_type=MESH)
        return carry

    def greet_depth(r, carry):
        @pl.when(jnp.logical_or(r != level, me != block))
        def _():
            pl.semaphore_signal(
                barrier, inc=1, device_id=(y * 32 + (r // 4) * 8 + block % 8, r % 4), device_id_type=MESH
            )
        return carry

    for r in range(1, SPLIT):
        pl.semaphore_signal(barrier, inc=1, device_id=(dp, (part + r) % SPLIT), device_id_type=MESH)
    lax.fori_loop(0, DEPTH, greet_depth, 0)
    lax.fori_loop(1, PLANE, greet_plane, 0)

    gain = ((1 << grade_ref[...]) - 1).astype(F32)
    scaled = score_ref[...] * LOG2E
    pack_tx[0] = scaled
    pack_tx[1] = gain
    pack_rx[part] = pack_tx[...]

    pl.semaphore_wait(barrier, PLANE - 1 + SPLIT - 1 + DEPTH - jnp.where(me == block, 1, 0))

    packs = []
    for r in range(1, SPLIT):
        copy = pltpu.make_async_remote_copy(
            src_ref=pack_tx, dst_ref=pack_rx.at[part], send_sem=pack_send.at[r], recv_sem=pack_recv.at[part],
            device_id=(dp, (part + r) % SPLIT), device_id_type=MESH,
        )
        copy.start()
        packs.append(copy)

    load.wait()

    def lay(i, carry):
        at = pl.multiple_of(i * 8, 8)
        for h in range(2):
            codes_tx[pl.ds(at, 8), h, :] = codes_in[pl.ds(at, 8), 128 * h:128 * h + 128]
        return carry

    whole = FEATURES // 8
    lax.fori_loop(0, whole, lay, 0, unroll=4)
    for h in range(2):
        codes_tx[8 * whole:FEATURES, h, :] = codes_in[8 * whole:FEATURES, 128 * h:128 * h + 128]
    codes_tx[FEATURES:FEATURES + 4] = jnp.zeros((4, 2, 128), I32)

    def first_feature(other):
        return (other * 175) // 8

    for c in range(CHUNKS):
        def send_codes(r, carry, c=c):
            other = (me + r) % PLANE
            pltpu.make_async_remote_copy(
                src_ref=codes_tx.at[pl.ds(first_feature(other) + PER * c, PER)], dst_ref=codes_rx.at[c, me],
                send_sem=code_send.at[c], recv_sem=code_recv.at[c],
                device_id=plane_peer(other), device_id_type=MESH,
            ).start()
            return carry

        lax.fori_loop(1, PLANE, send_codes, 0)
        codes_rx[c, me] = codes_tx[pl.ds(first_feature(me) + PER * c, PER)]

    sub = lax.broadcasted_iota(I32, (128, 128), 0)
    lane = lax.broadcasted_iota(I32, (128, 128), 1)
    lengths = jnp.broadcast_to(length_ref[...].astype(F32) * 0.125, (128, 128))
    ends = 8.0 * jnp.dot(
        jnp.where(lane <= sub, lengths, 0.0).astype(BF16), jnp.ones((128, 128), BF16), preferred_element_type=F32
    )
    lane_row = lax.broadcasted_iota(I32, (1, 128), 1).astype(F32)
    for b in range(TILES):
        rows = lane_row + 128.0 * b
        done = ends <= rows
        query[b:b + 1, :] = jnp.sum(jnp.where(done, 1.0, 0.0), axis=0, keepdims=True)
        first = jnp.max(jnp.where(done, ends, 0.0), axis=0, keepdims=True)
        discount[b:b + 1, :] = 1.0 / jnp.log2(rows - first + 2.0)

    pick_row = lax.broadcasted_iota(I32, (32, 256), 0)
    pick_lane = lax.broadcasted_iota(I32, (32, 256), 1)
    side = (pick_row < 24) == (pick_lane < 128)

    def spread(first, second, out):
        stack = jnp.concatenate([*pieces(first), second.astype(BF16)], axis=0)
        for b in range(TILES):
            pick = jnp.where(jnp.logical_and(side, pick_row % 8 == b), 1.0, 0.0).astype(BF16)
            out[128 * b:128 * b + 128, :] = lax.dot_general(
                stack, pick, (((0,), (0,)), ((), ())), preferred_element_type=F32
            )

    spread(discount[...], query[...], col_fixed)
    own_query = [query[pl.ds(2 * part + h, 1), :] for h in range(2)]
    own_discount = [discount[pl.ds(2 * part + h, 1), :] for h in range(2)]
    for b in range(TILES):
        for h in range(2):
            same[128 * b:128 * b + 128, 128 * h:128 * h + 128] = jnp.where(
                col_fixed[128 * b:128 * b + 128, 128:256] == own_query[h], 1.0, 0.0
            ).astype(BF16)

    for r in range(1, SPLIT):
        source = (part + r) % SPLIT
        pltpu.make_async_remote_copy(
            src_ref=pack_tx, dst_ref=pack_rx.at[source], send_sem=pack_send.at[r], recv_sem=pack_recv.at[source],
            device_id=(dp, source), device_id_type=MESH,
        ).wait_recv()
    score_all[...] = jnp.concatenate([pack_rx[s, 0] for s in range(SPLIT)], axis=0)
    gain_all[...] = jnp.concatenate([pack_rx[s, 1] for s in range(SPLIT)], axis=0)
    spread(score_all[...], gain_all[...], col_sent)

    def pair(a, own_score, own_gain, own_disc, own_q):
        at = slice(128 * a, 128 * a + 128)
        gap = own_gain - col_sent[at, 128:256]
        diff = own_score - col_sent[at, 0:128]
        power = jnp.exp2(jnp.where(gap < 0.0, -diff, diff))
        ratio = 1.0 / (1.0 + power)
        weight = jnp.where(own_q == col_fixed[at, 128:256], jnp.abs(own_disc - col_fixed[at, 0:128]), 0.0)
        return gap * (weight * ratio), power * ratio

    totals = []
    for b in range(TILES):
        row = slice(b, b + 1)
        total = None
        for a in range(max(0, b - REACH), b + 1):
            slope, _ = pair(a, score_all[row, :], gain_all[row, :], discount[row, :], query[row, :])
            push = over_rows(jnp.abs(slope)) * (1.0 if a == b else 2.0)
            total = push if total is None else total + push
        totals.append(jnp.sum(total, axis=0, keepdims=True))
    stack = jnp.concatenate([*pieces(jnp.concatenate(totals, axis=0)), jnp.zeros((8, 128), BF16)], axis=0)
    stack_row = lax.broadcasted_iota(I32, (32, 128), 0)
    query_total = jnp.zeros((32, 256), F32)
    for b in range(TILES):
        query_total += jnp.dot(
            jnp.where(stack_row % 8 == b, stack, jnp.zeros_like(stack)), same[128 * b:128 * b + 128, :],
            preferred_element_type=F32,
        )
    query_total = jnp.sum(query_total, axis=0, keepdims=True)
    factor = jnp.log2(1.0 + query_total) / jnp.maximum(query_total, 1.0)

    stats = []
    for h in range(2):
        slope_sum, curv_sum = jnp.zeros((8, 128), F32), jnp.zeros((8, 128), F32)
        own_score, own_gain = score_all[pl.ds(2 * part + h, 1), :], gain_all[pl.ds(2 * part + h, 1), :]
        for a in range(TILES):
            slope, other = pair(a, own_score, own_gain, own_discount[h], own_query[h])
            slope_sum += over_rows(slope)
            curv_sum += over_rows(jnp.abs(slope) * other)
        own_factor = factor[:, 128 * h:128 * h + 128]
        grad = -jnp.sum(slope_sum, axis=0, keepdims=True) * own_factor
        hess = jnp.sum(curv_sum, axis=0, keepdims=True) * own_factor
        grad_ref[h:h + 1, :] = grad
        hess_ref[h:h + 1, :] = hess
        node = node_ref[h:h + 1, :]
        for value in (grad, hess):
            for n in range(2):
                stats.append(jnp.where(node == n, value, 0.0))
    stat_tx[...] = jnp.concatenate(stats, axis=0)

    def send_stats(r, carry):
        pltpu.make_async_remote_copy(
            src_ref=stat_tx, dst_ref=stat_rx.at[me], send_sem=stat_send, recv_sem=stat_recv,
            device_id=plane_peer((me + r) % PLANE), device_id_type=MESH,
        ).start()
        return carry

    lax.fori_loop(1, PLANE, send_stats, 0)
    stat_rx[me] = stat_tx[...]
    wait_bytes(stat_rx.at[pl.ds(0, PLANE - 1)], stat_recv)

    def prepare(s, carry):
        value = stat_rx[s]
        high = value.astype(BF16).astype(F32)
        low = value - high
        for h in range(2):
            a, b = high[4 * h:4 * h + 4], low[4 * h:4 * h + 4]
            split[s, :, 128 * h:128 * h + 128] = jnp.concatenate([a, b, a, b], axis=0).astype(BF16)
        return carry

    lax.fori_loop(0, PLANE, prepare, 0, unroll=4)

    row16 = lax.broadcasted_iota(I32, (16, 128), 0)
    highs = [(row16 // 8 + 2 * i).astype(BF16) for i in range(QUAD // 2)]
    lows = [(row16 + 16 * i).astype(BF16) for i in range(LOW // 16)]
    one, zero = jnp.ones((16, 128), BF16), jnp.zeros((16, 128), BF16)
    start = (me * 175 * 32) % BINS

    def operands(c, base, s):
        left, right = [], []
        for f in range(QUAD):
            left_half, right_half = [], []
            for h in range(2):
                code = codes_rx[c, s, base + f, h:h + 1, :]
                low = jnp.broadcast_to(code & (LOW - 1), (16, 128)).astype(BF16)
                high = jnp.broadcast_to(code >> 6, (16, 128)).astype(BF16)
                stat = split[s, :, 128 * h:128 * h + 128]
                left_half.append(jnp.concatenate([jnp.where(high == x, stat, zero) for x in highs], axis=0))
                right_half.append(jnp.concatenate([jnp.where(low == x, one, zero) for x in lows], axis=0))
            left.append(jnp.concatenate(left_half, axis=1))
            right.append(jnp.concatenate(right_half, axis=1))
        return jnp.concatenate(left, axis=0), jnp.concatenate(right, axis=0)

    def quad(g, carry):
        c, base = g // 2, (g % 2) * QUAD

        @pl.when(g % 2 == 0)
        def _():
            wait_bytes(codes_rx.at[c, pl.ds(0, PLANE - 1)], code_recv.at[c])

        def step(i, total):
            both = [operands(c, base, i * STEP + u) for u in range(STEP)]
            return total + lax.dot_general(
                jnp.concatenate([a for a, _ in both], axis=1), jnp.concatenate([b for _, b in both], axis=1),
                (((1,), (1,)), ((), ())), preferred_element_type=F32,
            )

        table = lax.fori_loop(0, PLANE // STEP, step, jnp.zeros((QUAD * QUAD * 8, BINS), F32))
        for f in range(QUAD):
            for high in range(QUAD):
                r = 8 * (QUAD * f + high)
                both = table[r:r + 8, LOW * f:LOW * f + LOW]
                hist[g * QUAD + f, :, LOW * high:LOW * high + LOW] = both[0:4] + both[4:8]

        def send_window(k, carry):
            j = 3 * g - 2 + k

            @pl.when(j >= 0)
            def _():
                slot = (start + j * OWNED) // BINS
                mine = jnp.logical_and(me == block, j == place)

                @pl.when(mine)
                def _():
                    window_rx[level] = hist[pl.ds(slot, WINDOW)]

                @pl.when(jnp.logical_not(mine))
                def _():
                    pltpu.make_async_remote_copy(
                        src_ref=hist.at[pl.ds(slot, WINDOW)], dst_ref=window_rx.at[level],
                        send_sem=final_send.at[j], recv_sem=final_recv.at[level],
                        device_id=(me * 4 + j // 4, j % 4), device_id_type=MESH,
                    ).start()
            return carry

        lax.fori_loop(0, 3, send_window, 0)
        return carry

    lax.fori_loop(0, SLOTS // QUAD, quad, 0)

    def arrive(k, total):
        @pl.when(jnp.logical_or(me != block, k != level))
        def _():
            wait_bytes(window_rx.at[k], final_recv.at[k])
        return total + window_rx[k]

    total = lax.fori_loop(0, DEPTH, arrive, jnp.zeros((WINDOW, 4, BINS), F32))
    line = jnp.concatenate([total[i] for i in range(WINDOW)], axis=1)
    line = jnp.concatenate([line, line], axis=0) * (1.0 / 16.0)
    offset = ((block * 175 * 32) % BINS + place * OWNED) % BINS
    line = pltpu.roll(line, WINDOW * BINS - offset, 1)
    grad_hist_ref[...] = line[0:2, 0:OWNED]
    hess_hist_ref[...] = line[2:4, 0:OWNED]

    for copy in packs:
        copy.wait_send()
    for c in range(CHUNKS):
        wait_bytes(codes_rx.at[c, pl.ds(0, PLANE - 1)], code_send.at[c])
    wait_bytes(stat_rx.at[pl.ds(0, PLANE - 1)], stat_send)

    def sent(j, carry):
        @pl.when(jnp.logical_or(me != block, j != place))
        def _():
            wait_bytes(window_rx.at[j], final_send.at[j])
        return carry

    lax.fori_loop(0, DEPTH, sent, 0)


def shards(scores, grades, lengths, bin_codes, node_ids):
    vmem = pl.BlockSpec(memory_space=pltpu.VMEM)
    dma = pltpu.SemaphoreType.DMA
    rows = 2, 128
    grad, hess, grad_hist, hess_hist = pl.pallas_call(
        kernel,
        out_shape=[
            jax.ShapeDtypeStruct(rows, F32),
            jax.ShapeDtypeStruct(rows, F32),
            jax.ShapeDtypeStruct((2, OWNED), F32),
            jax.ShapeDtypeStruct((2, OWNED), F32),
        ],
        in_specs=[vmem, vmem, vmem, pl.BlockSpec(memory_space=pl.ANY), vmem],
        out_specs=[vmem] * 4,
        scratch_shapes=[
            pltpu.VMEM((FEATURES, 256), I32),
            pltpu.VMEM((FEATURES + 4, 2, 128), I32),
            pltpu.VMEM((CHUNKS, PLANE, PER, 2, 128), I32),
            pltpu.VMEM((2, 2, 128), F32),
            pltpu.VMEM((SPLIT, 2, 2, 128), F32),
            pltpu.VMEM((8, 128), F32),
            pltpu.VMEM((PLANE, 8, 128), F32),
            pltpu.VMEM((PLANE, 16, 256), BF16),
            pltpu.VMEM((8, 128), F32),
            pltpu.VMEM((8, 128), F32),
            pltpu.VMEM((8, 128), F32),
            pltpu.VMEM((8, 128), F32),
            pltpu.VMEM((128 * TILES, 256), F32),
            pltpu.VMEM((128 * TILES, 256), F32),
            pltpu.VMEM((128 * TILES, 256), BF16),
            pltpu.VMEM((SLOTS, 4, BINS), F32),
            pltpu.VMEM((DEPTH, WINDOW, 4, BINS), F32),
            dma,
            dma((SPLIT,)),
            dma((SPLIT,)),
            dma((CHUNKS,)),
            dma((CHUNKS,)),
            dma,
            dma,
            dma((DEPTH,)),
            dma((DEPTH,)),
        ],
        compiler_params=pltpu.CompilerParams(
            collective_id=0, has_side_effects=True, vmem_limit_bytes=40 * 2**20
        ),
        cost_estimate=pl.CostEstimate(flops=10**9, bytes_accessed=10**6, transcendentals=10**6),
    )(scores.reshape(rows), grades.reshape(rows), lengths, bin_codes, node_ids.reshape(rows))
    return grad.reshape(-1), hess.reshape(-1), grad_hist, hess_hist


def solution(mesh):
    rows = P(("dp", "qsplit"))
    bins = P(None, ("dp", "qsplit"))
    return jax.shard_map(
        shards,
        mesh=mesh,
        in_specs=(rows, rows, P("dp", None), bins, rows),
        out_specs=(rows, rows, bins, bins),
        check_vma=False,
    )
```

```python
import jax
import jax.numpy as jnp
from jax import lax
from jax.experimental import pallas as pl
from jax.experimental.pallas import tpu as pltpu
from jax.sharding import PartitionSpec as P

F32, I32, BF16 = jnp.float32, jnp.int32, jnp.bfloat16
MESH = pl.DeviceIdType.MESH

FEATURES = 700
BINS = 256
PLANE = 32
DEPTH = 16
SPLIT = 4
TILES = 8
REACH = 4
SLOTS = 24
QUAD = 4
LOW = BINS // QUAD
WINDOW = 3
WIDE = 384
OWNED = FEATURES * BINS // (PLANE * DEPTH)
LOG2E = 1.4426950408889634


def pieces(x):
    high = x.astype(BF16)
    rest = x - high.astype(F32)
    middle = rest.astype(BF16)
    return high, middle, (rest - middle.astype(F32)).astype(BF16)


def over_rows(x):
    return jnp.sum(x.reshape(x.shape[0] // 8, 8, x.shape[1]), axis=0)


def inverse(x):
    guess = pl.reciprocal(x, approx=True)
    return guess * (2.0 - x * guess)


def wait_bytes(ref, sem):
    pltpu.make_async_copy(ref, ref, sem).wait()


def feature_block(inner):
    x, core = inner // 2, inner % 2
    return 4 * (x % 2) + 2 * core + x // 2


def summing_device(eighth):
    x, core = 2 * (eighth % 2) + eighth // 4, (eighth // 2) % 2
    return 2 * x + core


def kernel(
    score_hbm, grade_hbm, length_hbm, codes_hbm, node_hbm,
    out_ref,
    score_ref, grade_ref, length_ref, codes_in, node_ref,
    codes_tx, codes_rx, pack_tx, pack_rx, stat_tx, stat_rx, split,
    query, discount, score_all, gain_all, col_fixed, col_sent, same, hist, window_tx, window_rx,
    load_sem, pack_send, pack_recv, code_send, code_recv, stat_send, stat_recv, final_send, final_recv,
):
    dp, part = lax.axis_index("dp"), lax.axis_index("qsplit")
    y, z_low, inner = dp // 32, (dp // 8) % 4, dp % 8
    me = y * 8 + inner
    level = z_low * 4 + part
    sums = y * 8 + feature_block(inner)
    block, place = dp // 4, (dp % 4) * 4 + part

    def plane_peer(other):
        return ((other // 8) * 32 + z_low * 8 + other % 8, part)

    def away(r):
        return (me + 1 + (r + 9) % (PLANE - 1)) % PLANE

    loads = []
    for i, (source, target) in enumerate((
        (score_hbm, score_ref), (grade_hbm, grade_ref), (length_hbm, length_ref), (node_hbm, node_ref),
        (codes_hbm, codes_in),
    )):
        loads.append(pltpu.make_async_copy(source, target, load_sem.at[i]))
        loads[-1].start()

    barrier = pltpu.get_barrier_semaphore()

    def greet_plane(r, carry):
        pl.semaphore_signal(barrier, inc=1, device_id=plane_peer(away(r)), device_id_type=MESH)
        return carry

    def greet_depth(r, carry):
        @pl.when(jnp.logical_or(r != level, sums != block))
        def _():
            pl.semaphore_signal(
                barrier, inc=1, device_id=(y * 32 + (r // 4) * 8 + summing_device(block % 8), r % 4), device_id_type=MESH
            )
        return carry

    for r in range(1, SPLIT):
        pl.semaphore_signal(barrier, inc=1, device_id=(dp, (part + r) % SPLIT), device_id_type=MESH)
    lax.fori_loop(0, DEPTH, greet_depth, 0)
    lax.fori_loop(0, PLANE - 1, greet_plane, 0)

    for load in loads[:4]:
        load.wait()

    gain = ((1 << grade_ref[...]) - 1).astype(F32)
    scaled = score_ref[...] * LOG2E
    pack_tx[0] = scaled
    pack_tx[1] = gain
    pack_rx[part] = pack_tx[...]

    pl.semaphore_wait(barrier, PLANE - 1 + SPLIT - 1 + DEPTH - jnp.where(sums == block, 1, 0))

    packs = []
    for r in range(1, SPLIT):
        copy = pltpu.make_async_remote_copy(
            src_ref=pack_tx, dst_ref=pack_rx.at[part], send_sem=pack_send.at[r], recv_sem=pack_recv.at[part],
            device_id=(dp, (part + r) % SPLIT), device_id_type=MESH,
        )
        copy.start()
        packs.append(copy)

    loads[4].wait()

    def lay(i, carry):
        at = pl.multiple_of(i * 8, 8)
        for h in range(2):
            codes_tx[pl.ds(at, 8), h, :] = codes_in[pl.ds(at, 8), 128 * h:128 * h + 128]
        return carry

    whole = FEATURES // 8
    lax.fori_loop(0, whole, lay, 0, unroll=4)
    for h in range(2):
        codes_tx[8 * whole:FEATURES, h, :] = codes_in[8 * whole:FEATURES, 128 * h:128 * h + 128]
    codes_tx[FEATURES:FEATURES + 4] = jnp.zeros((4, 2, 128), I32)

    def codes_for(other):
        first = ((other // 8) * 8 + feature_block(other % 8)) * 175 // 8
        return codes_tx.at[pl.ds(first, SLOTS)]

    def send_codes(r, carry):
        other = away(r)
        pltpu.make_async_remote_copy(
            src_ref=codes_for(other), dst_ref=codes_rx.at[me], send_sem=code_send, recv_sem=code_recv,
            device_id=plane_peer(other), device_id_type=MESH,
        ).start()
        return carry

    lax.fori_loop(0, PLANE - 1, send_codes, 0)
    codes_rx[me] = codes_for(me)[...]
    hist[...] = jnp.zeros_like(hist)

    sub = lax.broadcasted_iota(I32, (128, 128), 0)
    lane = lax.broadcasted_iota(I32, (128, 128), 1)
    lengths = jnp.broadcast_to(length_ref[...].astype(F32) * 0.125, (128, 128))
    ends = 8.0 * jnp.dot(
        jnp.where(lane <= sub, lengths, 0.0).astype(BF16), jnp.ones((128, 128), BF16), preferred_element_type=F32
    )
    lane_row = lax.broadcasted_iota(I32, (1, 128), 1).astype(F32)
    for b in range(TILES):
        rows = lane_row + 128.0 * b
        done = ends <= rows
        query[b:b + 1, :] = jnp.sum(jnp.where(done, 1.0, 0.0), axis=0, keepdims=True)
        first = jnp.max(jnp.where(done, ends, 0.0), axis=0, keepdims=True)
        discount[b:b + 1, :] = 1.0 / jnp.log2(rows - first + 2.0)

    pick_row = lax.broadcasted_iota(I32, (32, 256), 0)
    pick_lane = lax.broadcasted_iota(I32, (32, 256), 1)
    side = (pick_row < 24) == (pick_lane < 128)

    def spread(first, second, out):
        stack = jnp.concatenate([*pieces(first), second.astype(BF16)], axis=0)
        for b in range(TILES):
            pick = jnp.where(jnp.logical_and(side, pick_row % 8 == b), 1.0, 0.0).astype(BF16)
            out[128 * b:128 * b + 128, :] = lax.dot_general(
                stack, pick, (((0,), (0,)), ((), ())), preferred_element_type=F32
            )

    spread(discount[...], query[...], col_fixed)
    own_query = [query[pl.ds(2 * part + h, 1), :] for h in range(2)]
    own_discount = [discount[pl.ds(2 * part + h, 1), :] for h in range(2)]
    for b in range(TILES):
        for h in range(2):
            same[128 * b:128 * b + 128, 128 * h:128 * h + 128] = jnp.where(
                col_fixed[128 * b:128 * b + 128, 128:256] == own_query[h], 1.0, 0.0
            ).astype(BF16)

    for r in range(1, SPLIT):
        source = (part + r) % SPLIT
        pltpu.make_async_remote_copy(
            src_ref=pack_tx, dst_ref=pack_rx.at[source], send_sem=pack_send.at[r], recv_sem=pack_recv.at[source],
            device_id=(dp, source), device_id_type=MESH,
        ).wait_recv()
    score_all[...] = jnp.concatenate([pack_rx[s, 0] for s in range(SPLIT)], axis=0)
    gain_all[...] = jnp.concatenate([pack_rx[s, 1] for s in range(SPLIT)], axis=0)
    spread(score_all[...], gain_all[...], col_sent)

    def pair(a, own_score, own_gain, own_disc, own_q):
        at = slice(128 * a, 128 * a + 128)
        gap = own_gain - col_sent[at, 128:256]
        diff = own_score - col_sent[at, 0:128]
        power = jnp.exp2(jnp.where(gap < 0.0, -diff, diff))
        ratio = inverse(1.0 + power)
        weight = jnp.where(own_q == col_fixed[at, 128:256], jnp.abs(own_disc - col_fixed[at, 0:128]), 0.0)
        return gap * (weight * ratio), power * ratio

    totals = []
    for b in range(TILES):
        row = slice(b, b + 1)
        total = None
        for a in range(max(0, b - REACH), b + 1):
            slope, _ = pair(a, score_all[row, :], gain_all[row, :], discount[row, :], query[row, :])
            push = over_rows(jnp.abs(slope)) * (1.0 if a == b else 2.0)
            total = push if total is None else total + push
        totals.append(jnp.sum(total, axis=0, keepdims=True))
    stack = jnp.concatenate([*pieces(jnp.concatenate(totals, axis=0)), jnp.zeros((8, 128), BF16)], axis=0)
    stack_row = lax.broadcasted_iota(I32, (32, 128), 0)
    query_total = jnp.zeros((32, 256), F32)
    for b in range(TILES):
        query_total += jnp.dot(
            jnp.where(stack_row % 8 == b, stack, jnp.zeros_like(stack)), same[128 * b:128 * b + 128, :],
            preferred_element_type=F32,
        )
    query_total = jnp.sum(query_total, axis=0, keepdims=True)
    factor = jnp.log2(1.0 + query_total) / jnp.maximum(query_total, 1.0)

    stats = []
    for h in range(2):
        slope_sum, curv_sum = jnp.zeros((8, 128), F32), jnp.zeros((8, 128), F32)
        own_score, own_gain = score_all[pl.ds(2 * part + h, 1), :], gain_all[pl.ds(2 * part + h, 1), :]
        for a in range(TILES):
            slope, other = pair(a, own_score, own_gain, own_discount[h], own_query[h])
            slope_sum += over_rows(slope)
            curv_sum += over_rows(jnp.abs(slope) * other)
        own_factor = factor[:, 128 * h:128 * h + 128]
        grad = -jnp.sum(slope_sum, axis=0, keepdims=True) * own_factor
        hess = jnp.sum(curv_sum, axis=0, keepdims=True) * own_factor
        out_ref[4 + h:5 + h, 0:128] = grad
        out_ref[6 + h:7 + h, 0:128] = hess
        node = node_ref[h:h + 1, :]
        for value in (grad, hess):
            for n in range(2):
                stats.append(jnp.where(node == n, value, 0.0))
    stat_tx[...] = jnp.concatenate(stats, axis=0)

    def send_stats(r, carry):
        pltpu.make_async_remote_copy(
            src_ref=stat_tx, dst_ref=stat_rx.at[me], send_sem=stat_send, recv_sem=stat_recv,
            device_id=plane_peer(away(r)), device_id_type=MESH,
        ).start()
        return carry

    lax.fori_loop(0, PLANE - 1, send_stats, 0)
    stat_rx[me] = stat_tx[...]
    wait_bytes(stat_rx.at[pl.ds(0, PLANE - 1)], stat_recv)

    def prepare(s, carry):
        value = stat_rx[s]
        high = value.astype(BF16).astype(F32)
        low = value - high
        for h in range(2):
            a, b = high[4 * h:4 * h + 4], low[4 * h:4 * h + 4]
            split[s, :, 128 * h:128 * h + 128] = jnp.concatenate([a, b, a, b], axis=0).astype(BF16)
        return carry

    lax.fori_loop(0, PLANE, prepare, 0, unroll=4)

    row16 = lax.broadcasted_iota(I32, (16, 128), 0)
    highs = [(row16 // 8 + 2 * i).astype(BF16) for i in range(QUAD // 2)]
    lows = [(row16 + 16 * i).astype(BF16) for i in range(LOW // 16)]
    one, zero = jnp.ones((16, 128), BF16), jnp.zeros((16, 128), BF16)
    start = (sums * 175 * 32) % BINS

    def first_slot(j):
        return (start + j * OWNED) // BINS

    def slot_at(i):
        early = first_slot(4 * (i // 3)) + i % 3
        late = i - 9
        for k in (4, 8, 12):
            late = late + jnp.where(late >= first_slot(k), 3, 0)
        return jnp.where(i < 12, early, late)

    def quad_of(j):
        early = jnp.where(j >= 8, 2, j // 4)
        late = jnp.where(j < 4, 3, jnp.where(j < 12, 4, 5))
        return jnp.where(j % 4 == 0, early, late)

    def operands(slots, s):
        left, right = [], []
        for slot in slots:
            left_half, right_half = [], []
            for h in range(2):
                code = codes_rx[s, slot, h:h + 1, :]
                low = jnp.broadcast_to(code & (LOW - 1), (16, 128)).astype(BF16)
                high = jnp.broadcast_to(code >> 6, (16, 128)).astype(BF16)
                stat = split[s, :, 128 * h:128 * h + 128]
                left_half.append(jnp.concatenate([jnp.where(low == x, one, zero) for x in lows], axis=0))
                right_half.append(jnp.concatenate([jnp.where(high == x, stat, zero) for x in highs], axis=0))
            left.append(jnp.concatenate(left_half, axis=1))
            right.append(jnp.concatenate(right_half, axis=1))
        return jnp.concatenate(left, axis=0), jnp.concatenate(right, axis=0)

    wait_bytes(codes_rx.at[pl.ds(0, PLANE - 1)], code_recv)

    def quad(g, carry):
        slots = [slot_at(g * QUAD + f) for f in range(QUAD)]
        both = [operands(slots, s) for s in range(PLANE)]
        table = lax.dot_general(
            jnp.concatenate([a for a, _ in both], axis=1), jnp.concatenate([b for _, b in both], axis=1),
            (((1,), (1,)), ((), ())), preferred_element_type=F32,
        ).T
        for f in range(QUAD):
            for high in range(QUAD):
                r = 8 * (QUAD * f + high)
                halves = table[r:r + 8, LOW * f:LOW * f + LOW]
                hist[slots[f], :, LOW * high:LOW * high + LOW] = halves[0:4] + halves[4:8]

        def send_window(j, carry):
            @pl.when(quad_of(j) == g)
            def _():
                at = first_slot(j)
                line = jnp.concatenate([hist[at + i] for i in range(WINDOW)], axis=1)
                line = jnp.concatenate([line, line], axis=0)
                line = pltpu.roll(line, WINDOW * BINS - (start + j * OWNED) % BINS, 1)[0:4, 0:WIDE]
                mine = jnp.logical_and(sums == block, j == place)

                @pl.when(mine)
                def _():
                    window_rx[level] = line

                @pl.when(jnp.logical_not(mine))
                def _():
                    window_tx[j] = line
                    pltpu.make_async_remote_copy(
                        src_ref=window_tx.at[j], dst_ref=window_rx.at[level],
                        send_sem=final_send.at[j], recv_sem=final_recv.at[level],
                        device_id=(sums * 4 + j // 4, j % 4), device_id_type=MESH,
                    ).start()
            return carry

        lax.fori_loop(0, DEPTH, send_window, 0)
        return carry

    lax.fori_loop(0, SLOTS // QUAD, quad, 0)

    def arrive(k, total):
        @pl.when(jnp.logical_or(sums != block, k != level))
        def _():
            wait_bytes(window_rx.at[k], final_recv.at[k])
        return total + window_rx[k]

    total = lax.fori_loop(0, DEPTH, arrive, jnp.zeros((4, WIDE), F32))
    out_ref[0:4, :] = total * (1.0 / 16.0)

    for copy in packs:
        copy.wait_send()
    wait_bytes(codes_rx.at[pl.ds(0, PLANE - 1)], code_send)
    wait_bytes(stat_rx.at[pl.ds(0, PLANE - 1)], stat_send)

    def sent(j, carry):
        @pl.when(jnp.logical_or(sums != block, j != place))
        def _():
            wait_bytes(window_tx.at[j], final_send.at[j])
        return carry

    lax.fori_loop(0, DEPTH, sent, 0)


def unpack(packed_ref, grad_ref, hess_ref, grad_hist_ref, hess_hist_ref):
    grad_ref[...] = packed_ref[4:6, 0:128]
    hess_ref[...] = packed_ref[6:8, 0:128]
    grad_hist_ref[...] = packed_ref[0:2, 0:OWNED]
    hess_hist_ref[...] = packed_ref[2:4, 0:OWNED]


def shards(scores, grades, lengths, bin_codes, node_ids):
    vmem = pl.BlockSpec(memory_space=pltpu.VMEM)
    dma = pltpu.SemaphoreType.DMA
    rows = 2, 128
    packed = pl.pallas_call(
        kernel,
        out_shape=jax.ShapeDtypeStruct((8, WIDE), F32),
        in_specs=[pl.BlockSpec(memory_space=pl.ANY)] * 5,
        out_specs=vmem,
        scratch_shapes=[
            pltpu.VMEM(rows, F32),
            pltpu.VMEM(rows, I32),
            pltpu.VMEM((1, 128), I32),
            pltpu.VMEM((FEATURES, 256), I32),
            pltpu.VMEM(rows, I32),
            pltpu.VMEM((FEATURES + 4, 2, 128), I32),
            pltpu.VMEM((PLANE, SLOTS, 2, 128), I32),
            pltpu.VMEM((2, 2, 128), F32),
            pltpu.VMEM((SPLIT, 2, 2, 128), F32),
            pltpu.VMEM((8, 128), F32),
            pltpu.VMEM((PLANE, 8, 128), F32),
            pltpu.VMEM((PLANE, 16, 256), BF16),
            pltpu.VMEM((8, 128), F32),
            pltpu.VMEM((8, 128), F32),
            pltpu.VMEM((8, 128), F32),
            pltpu.VMEM((8, 128), F32),
            pltpu.VMEM((128 * TILES, 256), F32),
            pltpu.VMEM((128 * TILES, 256), F32),
            pltpu.VMEM((128 * TILES, 256), BF16),
            pltpu.VMEM((SLOTS, 4, BINS), F32),
            pltpu.VMEM((DEPTH, 4, WIDE), F32),
            pltpu.VMEM((DEPTH, 4, WIDE), F32),
            dma((5,)),
            dma((SPLIT,)),
            dma((SPLIT,)),
            dma,
            dma,
            dma,
            dma,
            dma((DEPTH,)),
            dma((DEPTH,)),
        ],
        compiler_params=pltpu.CompilerParams(
            collective_id=0, has_side_effects=True, vmem_limit_bytes=60 * 2**20
        ),
        cost_estimate=pl.CostEstimate(flops=10**9, bytes_accessed=10**6, transcendentals=10**6),
    )(scores.reshape(rows), grades.reshape(rows), lengths, bin_codes, node_ids.reshape(rows))
    grad, hess, grad_hist, hess_hist = pl.pallas_call(
        unpack,
        out_shape=[jax.ShapeDtypeStruct(shape, F32) for shape in (rows, rows, (2, OWNED), (2, OWNED))],
        in_specs=[vmem],
        out_specs=[vmem] * 4,
    )(packed)
    return grad.reshape(-1), hess.reshape(-1), grad_hist, hess_hist


def solution(mesh):
    rows = P(("dp", "qsplit"))
    bins = P(None, ("dp", "qsplit"))
    return jax.shard_map(
        shards,
        mesh=mesh,
        in_specs=(rows, rows, P("dp", None), bins, rows),
        out_specs=(rows, rows, bins, bins),
        check_vma=False,
    )
```

```python
import jax
import jax.numpy as jnp
from jax import lax
from jax.experimental import pallas as pl
from jax.experimental.pallas import tpu as pltpu
from jax.sharding import PartitionSpec as P

F32, I32, BF16 = jnp.float32, jnp.int32, jnp.bfloat16
MESH = pl.DeviceIdType.MESH

FEATURES = 700
BINS = 256
PLANE = 32
ROW = 8
DEPTH = 16
SPLIT = 4
TILES = 8
SLOTS = 24
EARLY = 21
QUAD = 4
LOW = BINS // QUAD
WINDOW = 4
WIDE = 384
OWNED = FEATURES * BINS // (PLANE * DEPTH)
LOG2E = 1.4426950408889634


def pieces(x):
    high = x.astype(BF16)
    rest = x - high.astype(F32)
    middle = rest.astype(BF16)
    return high, middle, (rest - middle.astype(F32)).astype(BF16)


def over_rows(x):
    return jnp.sum(x.reshape(x.shape[0] // 8, 8, x.shape[1]), axis=0)


def inverse(x):
    guess = pl.reciprocal(x, approx=True)
    return guess * (2.0 - x * guess)


def wait_bytes(ref, sem):
    pltpu.make_async_copy(ref, ref, sem).wait()


def feature_block(inner):
    x, core = inner // 2, inner % 2
    return 4 * (x % 2) + 2 * core + x // 2


def kernel(
    score_hbm, grade_hbm, length_hbm, codes_hbm, node_hbm,
    out_ref,
    score_ref, grade_ref, length_ref, codes_in, node_ref,
    codes_tx, codes_rx, pack_tx, pack_rx, stat_tx, stat_rx, split,
    query, discount, score_all, gain_all, col_fixed, col_sent, same, hist, window_rx,
    load_sem, pack_send, pack_recv, code_send, code_recv, stat_send, stat_recv, final_send, final_recv, ready,
):
    dp, part = lax.axis_index("dp"), lax.axis_index("qsplit")
    y, z_low, inner = dp // 32, (dp // 8) % 4, dp % 8
    level = z_low * 4 + part
    sums = y * 8 + feature_block(inner)
    block, place = dp // 4, (dp % 4) * 4 + part

    def near_peer(i):
        return 0, (inner + 1 + i) % ROW

    def far_peer(i):
        step = 1 + (1 + i // ROW) % 3
        return step, (inner + i) % ROW

    def device(peer):
        step, at = peer
        return (((y + step) % 4) * 32 + z_low * 8 + at, part)

    def slot(step):
        return ((4 - step) % 4) * ROW + inner

    loads = []
    for i, (source, target) in enumerate((
        (score_hbm, score_ref), (grade_hbm, grade_ref), (length_hbm, length_ref), (node_hbm, node_ref),
        (codes_hbm, codes_in),
    )):
        loads.append(pltpu.make_async_copy(source, target, load_sem.at[i]))
        loads[-1].start()

    barrier = pltpu.get_barrier_semaphore()

    def greet(peer):
        def body(i, carry):
            pl.semaphore_signal(barrier, inc=1, device_id=device(peer(i)), device_id_type=MESH)
            return carry
        return body

    for r in range(1, SPLIT):
        pl.semaphore_signal(barrier, inc=1, device_id=(dp, (part + r) % SPLIT), device_id_type=MESH)
    def neighbour(r):
        return (y * 32 + ((z_low + r) % 4) * 8 + inner, part)

    for r in range(1, 4):
        pl.semaphore_signal(barrier, inc=1, device_id=neighbour(r), device_id_type=MESH)
    lax.fori_loop(0, PLANE - ROW, greet(far_peer), 0)
    lax.fori_loop(0, ROW - 1, greet(near_peer), 0)

    for load in loads[:4]:
        load.wait()

    gain = ((1 << grade_ref[...]) - 1).astype(F32)
    scaled = score_ref[...] * LOG2E
    pack_tx[0] = scaled
    pack_tx[1] = gain
    pack_rx[0] = pack_tx[...]

    pl.semaphore_wait(barrier, PLANE - 1 + SPLIT - 1 + 3)

    packs = {}
    for r in range(1, SPLIT):
        packs[SPLIT - r] = pltpu.make_async_remote_copy(
            src_ref=pack_tx, dst_ref=pack_rx.at[SPLIT - r],
            send_sem=pack_send.at[SPLIT - r], recv_sem=pack_recv.at[SPLIT - r],
            device_id=(dp, (part + r) % SPLIT), device_id_type=MESH,
        )
    for r in (2, 1, 3):
        packs[r].start()

    loads[4].wait()

    def lay(i, carry):
        at = pl.multiple_of(i * 8, 8)
        for h in range(2):
            codes_tx[pl.ds(at, 8), h, :] = codes_in[pl.ds(at, 8), 128 * h:128 * h + 128]
        return carry

    whole = FEATURES // 8
    lax.fori_loop(0, whole, lay, 0, unroll=4)
    for h in range(2):
        codes_tx[8 * whole:FEATURES, h, :] = codes_in[8 * whole:FEATURES, 128 * h:128 * h + 128]
    codes_tx[FEATURES:FEATURES + 4] = jnp.zeros((4, 2, 128), I32)

    spans = pl.ds(0, EARLY), pl.ds(EARLY, SLOTS - EARLY)

    def codes_for(peer, late):
        step, at = peer
        first = (((y + step) % 4) * 8 + feature_block(at)) * 175 // 8
        return codes_tx.at[pl.ds(first + EARLY, SLOTS - EARLY) if late else pl.ds(first, EARLY)]

    def send_codes(late):
        def body(peer):
            def send(i, carry):
                to = peer(i)
                pltpu.make_async_remote_copy(
                    src_ref=codes_for(to, late), dst_ref=codes_rx.at[slot(to[0]), spans[late]],
                    send_sem=code_send.at[late], recv_sem=code_recv.at[late],
                    device_id=device(to), device_id_type=MESH,
                ).start()
                return carry
            return send

        lax.fori_loop(0, PLANE - ROW, body(far_peer), 0)
        lax.fori_loop(0, ROW - 1, body(near_peer), 0)
        codes_rx[inner, spans[late]] = codes_for((0, inner), late)[...]

    def wait_codes(late, sem):
        wait_bytes(codes_rx.at[pl.ds(0, PLANE - 1), spans[late]], sem.at[late])

    send_codes(0)

    sub = lax.broadcasted_iota(I32, (128, 128), 0)
    lane = lax.broadcasted_iota(I32, (128, 128), 1)
    lengths = jnp.broadcast_to(length_ref[...].astype(F32) * 0.125, (128, 128))
    ends = 8.0 * jnp.dot(
        jnp.where(lane <= sub, lengths, 0.0).astype(BF16), jnp.ones((128, 128), BF16), preferred_element_type=F32
    )
    lane_row = lax.broadcasted_iota(I32, (1, 128), 1).astype(F32)
    for b in range(TILES):
        rows = lane_row + 128.0 * ((2 * part + b) % TILES).astype(F32)
        done = ends <= rows
        query[b:b + 1, :] = jnp.sum(jnp.where(done, 1.0, 0.0), axis=0, keepdims=True)
        first = jnp.max(jnp.where(done, ends, 0.0), axis=0, keepdims=True)
        discount[b:b + 1, :] = 1.0 / jnp.log2(rows - first + 2.0)

    pick_row = lax.broadcasted_iota(I32, (32, 256), 0)
    pick_lane = lax.broadcasted_iota(I32, (32, 256), 1)
    side = (pick_row < 24) == (pick_lane < 128)

    def spread(first, second, out, tiles):
        stack = jnp.concatenate([*pieces(first), second.astype(BF16)], axis=0)
        for b in tiles:
            pick = jnp.where(jnp.logical_and(side, pick_row % 8 == b), 1.0, 0.0).astype(BF16)
            out[128 * b:128 * b + 128, :] = lax.dot_general(
                stack, pick, (((0,), (0,)), ((), ())), preferred_element_type=F32
            )

    spread(discount[...], query[...], col_fixed, range(TILES))
    for b in range(TILES):
        for h in range(2):
            same[128 * b:128 * b + 128, 128 * h:128 * h + 128] = jnp.where(
                col_fixed[128 * b:128 * b + 128, 128:256] == query[h:h + 1, :], 1.0, 0.0
            ).astype(BF16)

    near, far = (0, 1, 2, 3, 6, 7), (4, 5)
    blank = jnp.zeros((2, 128), F32)

    def gather(parts, tiles):
        score_all[...] = jnp.concatenate([pack_rx[r, 0] if r in parts else blank for r in range(SPLIT)], axis=0)
        gain_all[...] = jnp.concatenate([pack_rx[r, 1] if r in parts else blank for r in range(SPLIT)], axis=0)
        spread(score_all[...], gain_all[...], col_sent, tiles)

    def pair(a, b):
        at, row = slice(128 * a, 128 * a + 128), slice(b, b + 1)
        gap = gain_all[row, :] - col_sent[at, 128:256]
        diff = score_all[row, :] - col_sent[at, 0:128]
        power = jnp.exp2(jnp.where(gap < 0.0, -diff, diff))
        ratio = inverse(1.0 + power)
        weight = jnp.where(
            query[row, :] == col_fixed[at, 128:256], jnp.abs(discount[row, :] - col_fixed[at, 0:128]), 0.0
        )
        return gap * (weight * ratio), power * ratio

    nothing = jnp.zeros((8, 128), F32)
    slopes, curves, pushes = [nothing] * 2, [nothing] * 2, [nothing] * TILES

    def own_pairs(tiles):
        for h in range(2):
            for a in tiles:
                slope, other = pair(a, h)
                push = jnp.abs(slope)
                slopes[h] = slopes[h] + over_rows(slope)
                curves[h] = curves[h] + over_rows(push * other)
                pushes[h] = pushes[h] + over_rows(push) * (1.0 if a < 2 else 2.0)

    def other_pairs(a, b):
        slope, _ = pair(a, b)
        pushes[b] = pushes[b] + over_rows(jnp.abs(slope)) * (1.0 if a == b else 2.0)

    packs[1].wait_recv()
    packs[3].wait_recv()
    gather((0, 1, 3), near)
    own_pairs(near)
    for i, b in enumerate((2, 3, 6, 7)):
        for a in (2, 3, 6, 7)[:i + 1]:
            other_pairs(a, b)
    packs[2].wait_recv()

    for r in range(1, 4):
        pl.semaphore_signal(ready, inc=1, device_id=neighbour(r), device_id_type=MESH)
    gather(range(SPLIT), far)
    own_pairs(far)
    for b in far:
        for a in (2, 3, 6, 7, 4, 5)[:b + 1]:
            other_pairs(a, b)
    totals = [jnp.sum(x, axis=0, keepdims=True) for x in pushes]
    stack = jnp.concatenate([*pieces(jnp.concatenate(totals, axis=0)), jnp.zeros((8, 128), BF16)], axis=0)
    stack_row = lax.broadcasted_iota(I32, (32, 128), 0)
    query_total = jnp.zeros((32, 256), F32)
    for b in range(TILES):
        query_total += jnp.dot(
            jnp.where(stack_row % 8 == b, stack, jnp.zeros_like(stack)), same[128 * b:128 * b + 128, :],
            preferred_element_type=F32,
        )
    query_total = jnp.sum(query_total, axis=0, keepdims=True)
    factor = jnp.log2(1.0 + query_total) / jnp.maximum(query_total, 1.0)

    stats = []
    for h in range(2):
        own_factor = factor[:, 128 * h:128 * h + 128]
        grad = -jnp.sum(slopes[h], axis=0, keepdims=True) * own_factor
        hess = jnp.sum(curves[h], axis=0, keepdims=True) * own_factor
        out_ref[4 + h:5 + h, 0:128] = grad
        out_ref[6 + h:7 + h, 0:128] = hess
        node = node_ref[h:h + 1, :]
        for value in (grad, hess):
            for n in range(2):
                stats.append(jnp.where(node == n, value, 0.0))
    stat_tx[...] = jnp.concatenate(stats, axis=0)

    def send_stats(peer):
        def body(i, carry):
            to = peer(i)
            pltpu.make_async_remote_copy(
                src_ref=stat_tx, dst_ref=stat_rx.at[slot(to[0])], send_sem=stat_send, recv_sem=stat_recv,
                device_id=device(to), device_id_type=MESH,
            ).start()
            return carry
        return body

    lax.fori_loop(0, PLANE - ROW, send_stats(far_peer), 0)
    lax.fori_loop(0, ROW - 1, send_stats(near_peer), 0)
    stat_rx[inner] = stat_tx[...]
    send_codes(1)

    def prepare(s, carry):
        value = stat_rx[s]
        high = value.astype(BF16).astype(F32)
        low = value - high
        for h in range(2):
            a, b = high[4 * h:4 * h + 4], low[4 * h:4 * h + 4]
            split[s, :, 128 * h:128 * h + 128] = jnp.concatenate([a, b, a, b], axis=0).astype(BF16)
        return carry

    row16 = lax.broadcasted_iota(I32, (16, 128), 0)
    highs = [(row16 // 8 + 2 * i).astype(BF16) for i in range(QUAD // 2)]
    lows = [(row16 + 16 * i).astype(BF16) for i in range(LOW // 16)]
    one, zero = jnp.ones((16, 128), BF16), jnp.zeros((16, 128), BF16)
    start = (sums * 175 * 32) % BINS

    firsts = [(start + 4 * i * OWNED) // BINS for i in range(4)]

    def slot_at(i):
        first, second, late = firsts[0] + i, firsts[0] + 3, i - 16
        for k in range(4):
            first = jnp.where(i >= 3 * k, firsts[k] + i - 3 * k, first)
            second = jnp.where(i >= 12 + k, firsts[k] + 3, second)
            late = late + jnp.where(late >= firsts[k], 4, 0)
        return jnp.where(i < 12, first, jnp.where(i < 16, second, late))

    plan = [0, 3, 4, 4, 1, 3, 4, 4, 2, 3, 5, 5, 2, 3, 5, 5]

    def operands(slots, s):
        left, right = [], []
        for slot in slots:
            left_half, right_half = [], []
            for h in range(2):
                code = codes_rx[s, slot, h:h + 1, :]
                low = jnp.broadcast_to(code & (LOW - 1), (16, 128)).astype(BF16)
                high = jnp.broadcast_to(code >> 6, (16, 128)).astype(BF16)
                stat = split[s, :, 128 * h:128 * h + 128]
                left_half.append(jnp.concatenate([jnp.where(low == x, one, zero) for x in lows], axis=0))
                right_half.append(jnp.concatenate([jnp.where(high == x, stat, zero) for x in highs], axis=0))
            left.append(jnp.concatenate(left_half, axis=1))
            right.append(jnp.concatenate(right_half, axis=1))
        return jnp.concatenate(left, axis=0), jnp.concatenate(right, axis=0)

    wait_bytes(stat_rx.at[pl.ds(0, PLANE - 1)], stat_recv)
    lax.fori_loop(0, PLANE, prepare, 0, unroll=4)

    wait_codes(0, code_recv)
    pl.semaphore_wait(ready, 3)

    def quad(g, carry):
        slots = [slot_at(g * QUAD + f) for f in range(QUAD)]

        @pl.when(g == SLOTS // QUAD - 1)
        def _():
            wait_codes(1, code_recv)

        both = [operands(slots, s) for s in range(PLANE)]
        table = lax.dot_general(
            jnp.concatenate([a for a, _ in both], axis=1), jnp.concatenate([b for _, b in both], axis=1),
            (((1,), (1,)), ((), ())), preferred_element_type=F32,
        ).T
        for f in range(QUAD):
            for high in range(QUAD):
                r = 8 * (QUAD * f + high)
                halves = table[r:r + 8, LOW * f:LOW * f + LOW]
                hist[2 * slots[f] + high // 2, :, LOW * (high % 2):LOW * (high % 2) + LOW] = halves[0:4] + halves[4:8]

        for j in range(DEPTH):
            @pl.when(g == plan[j])
            def _(j=j):
                window = hist.at[pl.ds((start + j * OWNED) // 128, WINDOW)]
                mine = jnp.logical_and(sums == block, j == place)

                @pl.when(mine)
                def _():
                    window_rx[level] = window[...]

                @pl.when(jnp.logical_not(mine))
                def _():
                    pltpu.make_async_remote_copy(
                        src_ref=window, dst_ref=window_rx.at[level],
                        send_sem=final_send.at[j], recv_sem=final_recv.at[level],
                        device_id=(sums * 4 + j // 4, j % 4), device_id_type=MESH,
                    ).start()
        return carry

    lax.fori_loop(0, SLOTS // QUAD, quad, 0)

    def arrive(k, total):
        @pl.when(jnp.logical_or(sums != block, k != level))
        def _():
            wait_bytes(window_rx.at[k], final_recv.at[k])
        return total + window_rx[k]

    total = lax.fori_loop(0, DEPTH, arrive, jnp.zeros((WINDOW, 4, 128), F32))
    line = jnp.concatenate([total[i] for i in range(WINDOW)], axis=1) * (1.0 / 16.0)
    offset = ((block * 175 * 32) % BINS + place * OWNED) % 128
    out_ref[0:4, :] = pltpu.roll(jnp.concatenate([line, line], axis=0), WINDOW * 128 - offset, 1)[0:4, 0:WIDE]

    for copy in packs.values():
        copy.wait_send()
    wait_codes(0, code_send)
    wait_codes(1, code_send)
    wait_bytes(stat_rx.at[pl.ds(0, PLANE - 1)], stat_send)

    def sent(j, carry):
        @pl.when(jnp.logical_or(sums != block, j != place))
        def _():
            wait_bytes(window_rx.at[j], final_send.at[j])
        return carry

    lax.fori_loop(0, DEPTH, sent, 0)


def unpack(packed_ref, grad_ref, hess_ref, grad_hist_ref, hess_hist_ref):
    grad_ref[...] = packed_ref[4:6, 0:128]
    hess_ref[...] = packed_ref[6:8, 0:128]
    grad_hist_ref[...] = packed_ref[0:2, 0:OWNED]
    hess_hist_ref[...] = packed_ref[2:4, 0:OWNED]


def shards(scores, grades, lengths, bin_codes, node_ids):
    vmem = pl.BlockSpec(memory_space=pltpu.VMEM)
    dma = pltpu.SemaphoreType.DMA
    rows = 2, 128
    packed = pl.pallas_call(
        kernel,
        out_shape=jax.ShapeDtypeStruct((8, WIDE), F32),
        in_specs=[pl.BlockSpec(memory_space=pl.ANY)] * 5,
        out_specs=vmem,
        scratch_shapes=[
            pltpu.VMEM(rows, F32),
            pltpu.VMEM(rows, I32),
            pltpu.VMEM((1, 128), I32),
            pltpu.VMEM((FEATURES, 256), I32),
            pltpu.VMEM(rows, I32),
            pltpu.VMEM((FEATURES + 4, 2, 128), I32),
            pltpu.VMEM((PLANE, SLOTS, 2, 128), I32),
            pltpu.VMEM((2, 2, 128), F32),
            pltpu.VMEM((SPLIT, 2, 2, 128), F32),
            pltpu.VMEM((8, 128), F32),
            pltpu.VMEM((PLANE, 8, 128), F32),
            pltpu.VMEM((PLANE, 16, 256), BF16),
            pltpu.VMEM((8, 128), F32),
            pltpu.VMEM((8, 128), F32),
            pltpu.VMEM((8, 128), F32),
            pltpu.VMEM((8, 128), F32),
            pltpu.VMEM((128 * TILES, 256), F32),
            pltpu.VMEM((128 * TILES, 256), F32),
            pltpu.VMEM((128 * TILES, 256), BF16),
            pltpu.VMEM((2 * SLOTS, 4, 128), F32),
            pltpu.VMEM((DEPTH, WINDOW, 4, 128), F32),
            dma((5,)),
            dma((SPLIT,)),
            dma((SPLIT,)),
            dma((2,)),
            dma((2,)),
            dma,
            dma,
            dma((DEPTH,)),
            dma((DEPTH,)),
            pltpu.SemaphoreType.REGULAR,
        ],
        compiler_params=pltpu.CompilerParams(
            collective_id=0, has_side_effects=True, vmem_limit_bytes=60 * 2**20
        ),
        cost_estimate=pl.CostEstimate(flops=10**9, bytes_accessed=10**6, transcendentals=10**6),
    )(scores.reshape(rows), grades.reshape(rows), lengths, bin_codes, node_ids.reshape(rows))
    grad, hess, grad_hist, hess_hist = pl.pallas_call(
        unpack,
        out_shape=[jax.ShapeDtypeStruct(shape, F32) for shape in (rows, rows, (2, OWNED), (2, OWNED))],
        in_specs=[vmem],
        out_specs=[vmem] * 4,
    )(packed)
    return grad.reshape(-1), hess.reshape(-1), grad_hist, hess_hist


def solution(mesh):
    rows = P(("dp", "qsplit"))
    bins = P(None, ("dp", "qsplit"))
    return jax.shard_map(
        shards,
        mesh=mesh,
        in_specs=(rows, rows, P("dp", None), bins, rows),
        out_specs=(rows, rows, bins, bins),
        check_vma=False,
    )
```

```python
import jax
import jax.numpy as jnp
from jax import lax
from jax.experimental import pallas as pl
from jax.experimental.pallas import tpu as pltpu
from jax.sharding import PartitionSpec as P

F32, I32, BF16 = jnp.float32, jnp.int32, jnp.bfloat16
MESH = pl.DeviceIdType.MESH

FEATURES = 700
BINS = 256
PLANE = 32
ROW = 8
DEPTH = 16
SPLIT = 4
TILES = 8
SLOTS = 24
ORDER = (1, 3, 2, 0)
EARLY = 21
QUAD = 4
AHEAD = 4
LOW = BINS // QUAD
WINDOW = 4
WIDE = 384
OWNED = FEATURES * BINS // (PLANE * DEPTH)
LOG2E = 1.4426950408889634


def pieces(x):
    high = x.astype(BF16)
    rest = x - high.astype(F32)
    middle = rest.astype(BF16)
    return high, middle, (rest - middle.astype(F32)).astype(BF16)


def over_rows(x):
    return jnp.sum(x.reshape(x.shape[0] // 8, 8, x.shape[1]), axis=0)


def inverse(x):
    guess = pl.reciprocal(x, approx=True)
    return guess * (2.0 - x * guess)


def wait_bytes(ref, sem):
    pltpu.make_async_copy(ref, ref, sem).wait()


def feature_block(inner):
    x, core = inner // 2, inner % 2
    return 4 * (x % 2) + 2 * core + x // 2


def kernel(
    score_hbm, grade_hbm, length_hbm, codes_hbm, node_hbm,
    out_ref,
    score_ref, grade_ref, length_ref, codes_in, node_ref,
    codes_tx, codes_rx, pack_tx, pack_rx, stat_tx, stat_rx, split,
    query, discount, score_all, gain_all, col_fixed, col_sent, same, tables, hist, window_rx,
    load_sem, pack_send, pack_recv, code_send, code_recv, stat_send, stat_recv, final_send, final_recv, ready,
):
    dp, part = lax.axis_index("dp"), lax.axis_index("qsplit")
    y, z_low, inner = dp // 32, (dp // 8) % 4, dp % 8
    level = z_low * 4 + part
    sums = y * 8 + feature_block(inner)
    block, place = dp // 4, (dp % 4) * 4 + part

    def near_peer(i):
        return 0, (inner + 1 + i) % ROW

    def far_peer(i):
        step = 1 + (1 + i // ROW) % 3
        return step, (inner + i) % ROW

    def device(peer):
        step, at = peer
        return (((y + step) % 4) * 32 + z_low * 8 + at, part)

    def slot(step):
        return ((4 - step) % 4) * ROW + inner

    loads = []
    for i, (source, target) in enumerate((
        (score_hbm, score_ref), (grade_hbm, grade_ref), (length_hbm, length_ref), (node_hbm, node_ref),
        (codes_hbm, codes_in),
    )):
        loads.append(pltpu.make_async_copy(source, target, load_sem.at[i]))
        loads[-1].start()

    barrier = pltpu.get_barrier_semaphore()

    def greet(peer):
        def body(i, carry):
            pl.semaphore_signal(barrier, inc=1, device_id=device(peer(i)), device_id_type=MESH)
            return carry
        return body

    for r in range(1, SPLIT):
        pl.semaphore_signal(barrier, inc=1, device_id=(dp, (part + r) % SPLIT), device_id_type=MESH)
    def neighbour(r):
        return (y * 32 + ((z_low + r) % 4) * 8 + inner, part)

    for r in range(1, 4):
        pl.semaphore_signal(barrier, inc=1, device_id=neighbour(r), device_id_type=MESH)
    lax.fori_loop(0, PLANE - ROW, greet(far_peer), 0)
    lax.fori_loop(0, ROW - 1, greet(near_peer), 0)

    for load in loads[:4]:
        load.wait()

    gain = ((1 << grade_ref[...]) - 1).astype(F32)
    scaled = score_ref[...] * LOG2E
    pack_tx[0] = scaled
    pack_tx[1] = gain
    pack_rx[0] = pack_tx[...]

    pl.semaphore_wait(barrier, PLANE - 1 + SPLIT - 1 + 3)

    packs = {}
    for r in range(1, SPLIT):
        packs[SPLIT - r] = pltpu.make_async_remote_copy(
            src_ref=pack_tx, dst_ref=pack_rx.at[SPLIT - r],
            send_sem=pack_send.at[SPLIT - r], recv_sem=pack_recv.at[SPLIT - r],
            device_id=(dp, (part + r) % SPLIT), device_id_type=MESH,
        )
    for r in (2, 1, 3):
        packs[r].start()

    loads[4].wait()

    def lay(i, carry):
        at = pl.multiple_of(i * 8, 8)
        for h in range(2):
            codes_tx[pl.ds(at, 8), h, :] = codes_in[pl.ds(at, 8), 128 * h:128 * h + 128]
        return carry

    whole = FEATURES // 8
    lax.fori_loop(0, whole, lay, 0, unroll=4)
    for h in range(2):
        codes_tx[8 * whole:FEATURES, h, :] = codes_in[8 * whole:FEATURES, 128 * h:128 * h + 128]
    codes_tx[FEATURES:FEATURES + 4] = jnp.zeros((4, 2, 128), I32)

    spans = pl.ds(0, EARLY), pl.ds(EARLY, SLOTS - EARLY)

    def codes_for(peer, late):
        step, at = peer
        first = (((y + step) % 4) * 8 + feature_block(at)) * 175 // 8
        return codes_tx.at[pl.ds(first + EARLY, SLOTS - EARLY) if late else pl.ds(first, EARLY)]

    def send_codes(late):
        def body(peer):
            def send(i, carry):
                to = peer(i)
                pltpu.make_async_remote_copy(
                    src_ref=codes_for(to, late), dst_ref=codes_rx.at[slot(to[0]), spans[late]],
                    send_sem=code_send.at[late], recv_sem=code_recv.at[late],
                    device_id=device(to), device_id_type=MESH,
                ).start()
                return carry
            return send

        lax.fori_loop(0, PLANE - ROW, body(far_peer), 0)
        lax.fori_loop(0, ROW - 1, body(near_peer), 0)
        codes_rx[inner, spans[late]] = codes_for((0, inner), late)[...]

    def wait_codes(late, sem):
        wait_bytes(codes_rx.at[pl.ds(0, PLANE - 1), spans[late]], sem.at[late])

    send_codes(0)

    sub = lax.broadcasted_iota(I32, (128, 128), 0)
    lane = lax.broadcasted_iota(I32, (128, 128), 1)
    lengths = jnp.broadcast_to(length_ref[...].astype(F32) * 0.125, (128, 128))
    ends = 8.0 * jnp.dot(
        jnp.where(lane <= sub, lengths, 0.0).astype(BF16), jnp.ones((128, 128), BF16), preferred_element_type=F32
    )
    lane_row = lax.broadcasted_iota(I32, (1, 128), 1).astype(F32)
    for b in range(TILES):
        rows = lane_row + 128.0 * ((2 * part + b) % TILES).astype(F32)
        done = ends <= rows
        query[b:b + 1, :] = jnp.sum(jnp.where(done, 1.0, 0.0), axis=0, keepdims=True)
        first = jnp.max(jnp.where(done, ends, 0.0), axis=0, keepdims=True)
        discount[b:b + 1, :] = 1.0 / jnp.log2(rows - first + 2.0)

    pick_row = lax.broadcasted_iota(I32, (32, 256), 0)
    pick_lane = lax.broadcasted_iota(I32, (32, 256), 1)
    side = (pick_row < 24) == (pick_lane < 128)

    def spread(first, second, out, tiles):
        stack = jnp.concatenate([*pieces(first), second.astype(BF16)], axis=0)
        for b in tiles:
            pick = jnp.where(jnp.logical_and(side, pick_row % 8 == b), 1.0, 0.0).astype(BF16)
            out[128 * b:128 * b + 128, :] = lax.dot_general(
                stack, pick, (((0,), (0,)), ((), ())), preferred_element_type=F32
            )

    spread(discount[...], query[...], col_fixed, range(TILES))
    for b in range(TILES):
        for h in range(2):
            same[128 * b:128 * b + 128, 128 * h:128 * h + 128] = jnp.where(
                col_fixed[128 * b:128 * b + 128, 128:256] == query[h:h + 1, :], 1.0, 0.0
            ).astype(BF16)

    near, far = (0, 1, 2, 3, 6, 7), (4, 5)
    blank = jnp.zeros((2, 128), F32)

    def gather(parts, tiles):
        score_all[...] = jnp.concatenate([pack_rx[r, 0] if r in parts else blank for r in range(SPLIT)], axis=0)
        gain_all[...] = jnp.concatenate([pack_rx[r, 1] if r in parts else blank for r in range(SPLIT)], axis=0)
        spread(score_all[...], gain_all[...], col_sent, tiles)

    def pair(a, b):
        at, row = slice(128 * a, 128 * a + 128), slice(b, b + 1)
        gap = gain_all[row, :] - col_sent[at, 128:256]
        diff = score_all[row, :] - col_sent[at, 0:128]
        power = jnp.exp2(jnp.where(gap < 0.0, -diff, diff))
        ratio = inverse(1.0 + power)
        weight = jnp.where(
            query[row, :] == col_fixed[at, 128:256], jnp.abs(discount[row, :] - col_fixed[at, 0:128]), 0.0
        )
        return gap * (weight * ratio), power * ratio

    nothing = jnp.zeros((8, 128), F32)
    slopes, curves, pushes = [nothing] * 2, [nothing] * 2, [nothing] * TILES

    def own_pairs(tiles):
        for h in range(2):
            for a in tiles:
                slope, other = pair(a, h)
                push = jnp.abs(slope)
                slopes[h] = slopes[h] + over_rows(slope)
                curves[h] = curves[h] + over_rows(push * other)
                pushes[h] = pushes[h] + over_rows(push) * (1.0 if a < 2 else 2.0)

    def other_pairs(a, b):
        slope, _ = pair(a, b)
        pushes[b] = pushes[b] + over_rows(jnp.abs(slope)) * (1.0 if a == b else 2.0)

    packs[1].wait_recv()
    packs[3].wait_recv()
    gather((0, 1, 3), near)
    own_pairs(near)
    for i, b in enumerate((2, 3, 6, 7)):
        for a in (2, 3, 6, 7)[:i + 1]:
            other_pairs(a, b)
    packs[2].wait_recv()

    for r in range(1, 4):
        pl.semaphore_signal(ready, inc=1, device_id=neighbour(r), device_id_type=MESH)
    gather(range(SPLIT), far)
    own_pairs(far)
    for b in far:
        for a in (2, 3, 6, 7, 4, 5)[:b + 1]:
            other_pairs(a, b)
    totals = [jnp.sum(x, axis=0, keepdims=True) for x in pushes]
    stack = jnp.concatenate([*pieces(jnp.concatenate(totals, axis=0)), jnp.zeros((8, 128), BF16)], axis=0)
    stack_row = lax.broadcasted_iota(I32, (32, 128), 0)
    query_total = jnp.zeros((32, 256), F32)
    for b in range(TILES):
        query_total += jnp.dot(
            jnp.where(stack_row % 8 == b, stack, jnp.zeros_like(stack)), same[128 * b:128 * b + 128, :],
            preferred_element_type=F32,
        )
    query_total = jnp.sum(query_total, axis=0, keepdims=True)
    factor = jnp.log2(1.0 + query_total) / jnp.maximum(query_total, 1.0)

    stats = []
    for h in range(2):
        own_factor = factor[:, 128 * h:128 * h + 128]
        grad = -jnp.sum(slopes[h], axis=0, keepdims=True) * own_factor
        hess = jnp.sum(curves[h], axis=0, keepdims=True) * own_factor
        out_ref[4 + h:5 + h, 0:128] = grad
        out_ref[6 + h:7 + h, 0:128] = hess
        node = node_ref[h:h + 1, :]
        for value in (grad, hess):
            for n in range(2):
                stats.append(jnp.where(node == n, value, 0.0))
    stat_tx[...] = jnp.concatenate(stats, axis=0)

    def send_stats(peer, far):
        def body(i, carry):
            to = peer(i)
            pltpu.make_async_remote_copy(
                src_ref=stat_tx, dst_ref=stat_rx.at[slot(to[0])], send_sem=stat_send, recv_sem=stat_recv.at[far],
                device_id=device(to), device_id_type=MESH,
            ).start()
            return carry
        return body

    lax.fori_loop(0, PLANE - ROW, send_stats(far_peer, 1), 0)
    lax.fori_loop(0, ROW - 1, send_stats(near_peer, 0), 0)
    stat_rx[inner] = stat_tx[...]
    send_codes(1)

    def prepare(s, carry):
        value = stat_rx[s]
        high = value.astype(BF16).astype(F32)
        low = value - high
        for h in range(2):
            a, b = high[4 * h:4 * h + 4], low[4 * h:4 * h + 4]
            split[s, :, 128 * h:128 * h + 128] = jnp.concatenate([a, b, a, b], axis=0).astype(BF16)
        return carry

    row16 = lax.broadcasted_iota(I32, (16, 128), 0)
    highs = [(row16 // 8 + 2 * i).astype(BF16) for i in range(QUAD // 2)]
    lows = [(row16 + 16 * i).astype(BF16) for i in range(LOW // 16)]
    one, zero = jnp.ones((16, 128), BF16), jnp.zeros((16, 128), BF16)
    start = (sums * 175 * 32) % BINS

    firsts = [(start + 4 * i * OWNED) // BINS for i in range(4)]

    def slot_at(i):
        first, second, late = i, firsts[0] + 3, i - 16
        for k in range(4):
            first = jnp.where(i >= 3 * k, firsts[ORDER[k]] + i - 3 * k, first)
            second = jnp.where(i >= 12 + k, firsts[k] + 3, second)
            late = late + jnp.where(late >= firsts[k], 4, 0)
        return jnp.where(i < 12, first, jnp.where(i < 16, second, late))

    plan = [2, 3, 4, 4, 0, 3, 4, 4, 2, 3, 5, 5, 1, 3, 5, 5]

    def operands(slots, s):
        left, right = [], []
        for slot in slots:
            left_half, right_half = [], []
            for h in range(2):
                code = codes_rx[s, slot, h:h + 1, :]
                low = jnp.broadcast_to(code & (LOW - 1), (16, 128)).astype(BF16)
                high = jnp.broadcast_to(code >> 6, (16, 128)).astype(BF16)
                stat = split[s, :, 128 * h:128 * h + 128]
                left_half.append(jnp.concatenate([jnp.where(low == x, one, zero) for x in lows], axis=0))
                right_half.append(jnp.concatenate([jnp.where(high == x, stat, zero) for x in highs], axis=0))
            left.append(jnp.concatenate(left_half, axis=1))
            right.append(jnp.concatenate(right_half, axis=1))
        return jnp.concatenate(left, axis=0), jnp.concatenate(right, axis=0)

    def product(slots, sources):
        both = [operands(slots, s) for s in sources]
        return lax.dot_general(
            jnp.concatenate([a for a, _ in both], axis=1), jnp.concatenate([b for _, b in both], axis=1),
            (((1,), (1,)), ((), ())), preferred_element_type=F32,
        )

    def slots_of(g):
        return [slot_at(g * QUAD + f) for f in range(QUAD)]

    def near_quad(g, carry):
        tables[g] = product(slots_of(g), range(ROW))
        return carry

    def far_quad(g, carry):
        slots = slots_of(g)
        finish(g, slots, tables[g] + product(slots, range(ROW, PLANE)))
        return carry

    def whole_quad(g, carry):
        slots = slots_of(g)

        @pl.when(g == SLOTS // QUAD - 1)
        def _():
            wait_codes(1, code_recv)

        finish(g, slots, product(slots, range(PLANE)))
        return carry

    def finish(g, slots, table):
        table = table.T
        for f in range(QUAD):
            for high in range(QUAD):
                r = 8 * (QUAD * f + high)
                halves = table[r:r + 8, LOW * f:LOW * f + LOW]
                hist[2 * slots[f] + high // 2, :, LOW * (high % 2):LOW * (high % 2) + LOW] = halves[0:4] + halves[4:8]

        for j in range(DEPTH):
            @pl.when(g == plan[j])
            def _(j=j):
                window = hist.at[pl.ds((start + j * OWNED) // 128, WINDOW)]
                mine = jnp.logical_and(sums == block, j == place)

                @pl.when(mine)
                def _():
                    window_rx[level] = window[...]

                @pl.when(jnp.logical_not(mine))
                def _():
                    pltpu.make_async_remote_copy(
                        src_ref=window, dst_ref=window_rx.at[level],
                        send_sem=final_send.at[j], recv_sem=final_recv.at[level],
                        device_id=(sums * 4 + j // 4, j % 4), device_id_type=MESH,
                    ).start()

    wait_codes(0, code_recv)
    wait_bytes(stat_rx.at[pl.ds(0, ROW - 1)], stat_recv.at[0])
    lax.fori_loop(0, ROW, prepare, 0, unroll=4)
    lax.fori_loop(0, AHEAD, near_quad, 0)
    wait_bytes(stat_rx.at[pl.ds(0, PLANE - ROW)], stat_recv.at[1])
    lax.fori_loop(ROW, PLANE, prepare, 0, unroll=4)
    pl.semaphore_wait(ready, 3)
    lax.fori_loop(0, AHEAD, far_quad, 0)
    lax.fori_loop(AHEAD, SLOTS // QUAD, whole_quad, 0)

    def arrive(k, total):
        @pl.when(jnp.logical_or(sums != block, k != level))
        def _():
            wait_bytes(window_rx.at[k], final_recv.at[k])
        return total + window_rx[k]

    total = lax.fori_loop(0, DEPTH, arrive, jnp.zeros((WINDOW, 4, 128), F32))
    line = jnp.concatenate([total[i] for i in range(WINDOW)], axis=1) * (1.0 / 16.0)
    offset = ((block * 175 * 32) % BINS + place * OWNED) % 128
    out_ref[0:4, :] = pltpu.roll(jnp.concatenate([line, line], axis=0), WINDOW * 128 - offset, 1)[0:4, 0:WIDE]

    for copy in packs.values():
        copy.wait_send()
    wait_codes(0, code_send)
    wait_codes(1, code_send)
    wait_bytes(stat_rx.at[pl.ds(0, PLANE - 1)], stat_send)

    def sent(j, carry):
        @pl.when(jnp.logical_or(sums != block, j != place))
        def _():
            wait_bytes(window_rx.at[j], final_send.at[j])
        return carry

    lax.fori_loop(0, DEPTH, sent, 0)


def unpack(packed_ref, grad_ref, hess_ref, grad_hist_ref, hess_hist_ref):
    grad_ref[...] = packed_ref[4:6, 0:128]
    hess_ref[...] = packed_ref[6:8, 0:128]
    grad_hist_ref[...] = packed_ref[0:2, 0:OWNED]
    hess_hist_ref[...] = packed_ref[2:4, 0:OWNED]


def shards(scores, grades, lengths, bin_codes, node_ids):
    vmem = pl.BlockSpec(memory_space=pltpu.VMEM)
    dma = pltpu.SemaphoreType.DMA
    rows = 2, 128
    packed = pl.pallas_call(
        kernel,
        out_shape=jax.ShapeDtypeStruct((8, WIDE), F32),
        in_specs=[pl.BlockSpec(memory_space=pl.ANY)] * 5,
        out_specs=vmem,
        scratch_shapes=[
            pltpu.VMEM(rows, F32),
            pltpu.VMEM(rows, I32),
            pltpu.VMEM((1, 128), I32),
            pltpu.VMEM((FEATURES, 256), I32),
            pltpu.VMEM(rows, I32),
            pltpu.VMEM((FEATURES + 4, 2, 128), I32),
            pltpu.VMEM((PLANE, SLOTS, 2, 128), I32),
            pltpu.VMEM((2, 2, 128), F32),
            pltpu.VMEM((SPLIT, 2, 2, 128), F32),
            pltpu.VMEM((8, 128), F32),
            pltpu.VMEM((PLANE, 8, 128), F32),
            pltpu.VMEM((PLANE, 16, 256), BF16),
            pltpu.VMEM((8, 128), F32),
            pltpu.VMEM((8, 128), F32),
            pltpu.VMEM((8, 128), F32),
            pltpu.VMEM((8, 128), F32),
            pltpu.VMEM((128 * TILES, 256), F32),
            pltpu.VMEM((128 * TILES, 256), F32),
            pltpu.VMEM((128 * TILES, 256), BF16),
            pltpu.VMEM((AHEAD, QUAD * LOW, QUAD * QUAD * 8), F32),
            pltpu.VMEM((2 * SLOTS, 4, 128), F32),
            pltpu.VMEM((DEPTH, WINDOW, 4, 128), F32),
            dma((5,)),
            dma((SPLIT,)),
            dma((SPLIT,)),
            dma((2,)),
            dma((2,)),
            dma,
            dma((2,)),
            dma((DEPTH,)),
            dma((DEPTH,)),
            pltpu.SemaphoreType.REGULAR,
        ],
        compiler_params=pltpu.CompilerParams(
            collective_id=0, has_side_effects=True, vmem_limit_bytes=60 * 2**20
        ),
        cost_estimate=pl.CostEstimate(flops=10**9, bytes_accessed=10**6, transcendentals=10**6),
    )(scores.reshape(rows), grades.reshape(rows), lengths, bin_codes, node_ids.reshape(rows))
    grad, hess, grad_hist, hess_hist = pl.pallas_call(
        unpack,
        out_shape=[jax.ShapeDtypeStruct(shape, F32) for shape in (rows, rows, (2, OWNED), (2, OWNED))],
        in_specs=[vmem],
        out_specs=[vmem] * 4,
    )(packed)
    return grad.reshape(-1), hess.reshape(-1), grad_hist, hess_hist


def solution(mesh):
    rows = P(("dp", "qsplit"))
    bins = P(None, ("dp", "qsplit"))
    return jax.shard_map(
        shards,
        mesh=mesh,
        in_specs=(rows, rows, P("dp", None), bins, rows),
        out_specs=(rows, rows, bins, bins),
        check_vma=False,
    )
```

```python
import jax
import jax.numpy as jnp
from jax import lax
from jax.experimental import pallas as pl
from jax.experimental.pallas import tpu as pltpu
from jax.sharding import PartitionSpec as P

F32, I32, BF16 = jnp.float32, jnp.int32, jnp.bfloat16
MESH = pl.DeviceIdType.MESH

FEATURES = 700
BINS = 256
PLANE = 32
ROW = 8
DEPTH = 16
SPLIT = 4
TILES = 8
SLOTS = 24
ORDER = (1, 3, 2, 0)
EARLY = 21
QUAD = 4
AHEAD = 4
LOW = BINS // QUAD
WINDOW = 4
WIDE = 384
OWNED = FEATURES * BINS // (PLANE * DEPTH)
LOG2E = 1.4426950408889634


def pieces(x):
    high = x.astype(BF16)
    rest = x - high.astype(F32)
    middle = rest.astype(BF16)
    return high, middle, (rest - middle.astype(F32)).astype(BF16)


def over_rows(x):
    return jnp.sum(x.reshape(x.shape[0] // 8, 8, x.shape[1]), axis=0)


def inverse(x):
    guess = pl.reciprocal(x, approx=True)
    return guess * (2.0 - x * guess)


def wait_bytes(ref, sem):
    pltpu.make_async_copy(ref, ref, sem).wait()


def feature_block(inner):
    x, core = inner // 2, inner % 2
    return 4 * (x % 2) + 2 * core + x // 2


def kernel(
    score_hbm, grade_hbm, length_hbm, codes_hbm, node_hbm,
    out_ref,
    score_ref, grade_ref, length_ref, codes_in, node_ref,
    codes_tx, codes_rx, pack_tx, pack_rx, stat_tx, stat_rx, split,
    query, discount, score_all, gain_all, col_fixed, col_sent, same, tables, hist, window_rx,
    load_sem, pack_send, pack_recv, code_send, code_recv, stat_send, stat_recv, final_send, final_recv, ready,
):
    dp, part = lax.axis_index("dp"), lax.axis_index("qsplit")
    y, z_low, inner = dp // 32, (dp // 8) % 4, dp % 8
    level = z_low * 4 + part
    sums = y * 8 + feature_block(inner)
    block, place = dp // 4, (dp % 4) * 4 + part

    def near_peer(i):
        return 0, (inner + 1 + i) % ROW

    def far_peer(i):
        step = 1 + (1 + i // ROW) % 3
        return step, (inner + i) % ROW

    def device(peer):
        step, at = peer
        return (((y + step) % 4) * 32 + z_low * 8 + at, part)

    def slot(step):
        return ((4 - step) % 4) * ROW + inner

    barrier = pltpu.get_barrier_semaphore()

    def greet(peer):
        def body(i, carry):
            pl.semaphore_signal(barrier, inc=1, device_id=device(peer(i)), device_id_type=MESH)
            return carry
        return body

    for r in (2, 1, 3):
        pl.semaphore_signal(barrier, inc=1, device_id=(dp, (part + r) % SPLIT), device_id_type=MESH)
    def neighbour(r):
        return (y * 32 + ((z_low + r) % 4) * 8 + inner, part)

    for r in range(1, 4):
        pl.semaphore_signal(barrier, inc=1, device_id=neighbour(r), device_id_type=MESH)
    loads = []
    for i, (source, target) in enumerate((
        (score_hbm, score_ref), (grade_hbm, grade_ref), (length_hbm, length_ref), (node_hbm, node_ref),
        (codes_hbm, codes_in),
    )):
        loads.append(pltpu.make_async_copy(source, target, load_sem.at[i]))
        loads[-1].start()

    lax.fori_loop(0, PLANE - ROW, greet(far_peer), 0)
    lax.fori_loop(0, ROW - 1, greet(near_peer), 0)

    for load in loads[:4]:
        load.wait()

    gain = ((1 << grade_ref[...]) - 1).astype(F32)
    scaled = score_ref[...] * LOG2E
    pack_tx[0] = scaled
    pack_tx[1] = gain
    pack_rx[0] = pack_tx[...]

    pl.semaphore_wait(barrier, PLANE - 1 + SPLIT - 1 + 3)

    packs = {}
    for r in range(1, SPLIT):
        packs[SPLIT - r] = pltpu.make_async_remote_copy(
            src_ref=pack_tx, dst_ref=pack_rx.at[SPLIT - r],
            send_sem=pack_send.at[SPLIT - r], recv_sem=pack_recv.at[SPLIT - r],
            device_id=(dp, (part + r) % SPLIT), device_id_type=MESH,
        )
    for r in (2, 1, 3):
        packs[r].start()

    loads[4].wait()

    def lay(i, carry):
        at = pl.multiple_of(i * 8, 8)
        for h in range(2):
            codes_tx[pl.ds(at, 8), h, :] = codes_in[pl.ds(at, 8), 128 * h:128 * h + 128]
        return carry

    whole = FEATURES // 8
    lax.fori_loop(0, whole, lay, 0, unroll=4)
    for h in range(2):
        codes_tx[8 * whole:FEATURES, h, :] = codes_in[8 * whole:FEATURES, 128 * h:128 * h + 128]
    codes_tx[FEATURES:FEATURES + 4] = jnp.zeros((4, 2, 128), I32)

    spans = pl.ds(0, EARLY), pl.ds(EARLY, SLOTS - EARLY)

    def codes_for(peer, late):
        step, at = peer
        first = (((y + step) % 4) * 8 + feature_block(at)) * 175 // 8
        return codes_tx.at[pl.ds(first + EARLY, SLOTS - EARLY) if late else pl.ds(first, EARLY)]

    def send_codes(late):
        def body(peer, far):
            def send(i, carry):
                to = peer(i)
                pltpu.make_async_remote_copy(
                    src_ref=codes_for(to, late), dst_ref=codes_rx.at[slot(to[0]), spans[late]],
                    send_sem=code_send.at[2 * late + far], recv_sem=code_recv.at[2 * late + far],
                    device_id=device(to), device_id_type=MESH,
                ).start()
                return carry
            return send

        lax.fori_loop(0, ROW - 1, body(near_peer, 0), 0)
        lax.fori_loop(0, PLANE - ROW, body(far_peer, 1), 0)
        codes_rx[inner, spans[late]] = codes_for((0, inner), late)[...]

    def wait_codes(late, far, sem):
        wait_bytes(codes_rx.at[pl.ds(0, PLANE - ROW if far else ROW - 1), spans[late]], sem.at[2 * late + far])

    send_codes(0)

    sub = lax.broadcasted_iota(I32, (128, 128), 0)
    lane = lax.broadcasted_iota(I32, (128, 128), 1)
    lengths = jnp.broadcast_to(length_ref[...].astype(F32) * 0.125, (128, 128))
    ends = 8.0 * jnp.dot(
        jnp.where(lane <= sub, lengths, 0.0).astype(BF16), jnp.ones((128, 128), BF16), preferred_element_type=F32
    )
    lane_row = lax.broadcasted_iota(I32, (1, 128), 1).astype(F32)
    for b in range(TILES):
        rows = lane_row + 128.0 * ((2 * part + b) % TILES).astype(F32)
        done = ends <= rows
        query[b:b + 1, :] = jnp.sum(jnp.where(done, 1.0, 0.0), axis=0, keepdims=True)
        first = jnp.max(jnp.where(done, ends, 0.0), axis=0, keepdims=True)
        discount[b:b + 1, :] = 1.0 / jnp.log2(rows - first + 2.0)

    pick_row = lax.broadcasted_iota(I32, (32, 256), 0)
    pick_lane = lax.broadcasted_iota(I32, (32, 256), 1)
    side = (pick_row < 24) == (pick_lane < 128)

    def spread(first, second, out, tiles):
        stack = jnp.concatenate([*pieces(first), second.astype(BF16)], axis=0)
        for b in tiles:
            pick = jnp.where(jnp.logical_and(side, pick_row % 8 == b), 1.0, 0.0).astype(BF16)
            out[128 * b:128 * b + 128, :] = lax.dot_general(
                stack, pick, (((0,), (0,)), ((), ())), preferred_element_type=F32
            )

    spread(discount[...], query[...], col_fixed, range(TILES))
    for b in range(TILES):
        for h in range(2):
            same[128 * b:128 * b + 128, 128 * h:128 * h + 128] = jnp.where(
                col_fixed[128 * b:128 * b + 128, 128:256] == query[h:h + 1, :], 1.0, 0.0
            ).astype(BF16)

    near, far = (0, 1, 2, 3, 6, 7), (4, 5)
    blank = jnp.zeros((2, 128), F32)

    def gather(parts, tiles):
        score_all[...] = jnp.concatenate([pack_rx[r, 0] if r in parts else blank for r in range(SPLIT)], axis=0)
        gain_all[...] = jnp.concatenate([pack_rx[r, 1] if r in parts else blank for r in range(SPLIT)], axis=0)
        spread(score_all[...], gain_all[...], col_sent, tiles)

    def pair(a, b):
        at, row = slice(128 * a, 128 * a + 128), slice(b, b + 1)
        gap = gain_all[row, :] - col_sent[at, 128:256]
        diff = score_all[row, :] - col_sent[at, 0:128]
        power = jnp.exp2(jnp.where(gap < 0.0, -diff, diff))
        ratio = inverse(1.0 + power)
        weight = jnp.where(
            query[row, :] == col_fixed[at, 128:256], jnp.abs(discount[row, :] - col_fixed[at, 0:128]), 0.0
        )
        return gap * (weight * ratio), power * ratio

    nothing = jnp.zeros((8, 128), F32)
    slopes, curves, pushes = [nothing] * 2, [nothing] * 2, [nothing] * TILES

    def own_pairs(tiles):
        for h in range(2):
            for a in tiles:
                slope, other = pair(a, h)
                push = jnp.abs(slope)
                slopes[h] = slopes[h] + over_rows(slope)
                curves[h] = curves[h] + over_rows(push * other)
                pushes[h] = pushes[h] + over_rows(push) * (1.0 if a < 2 else 2.0)

    def other_pairs(a, b):
        slope, _ = pair(a, b)
        pushes[b] = pushes[b] + over_rows(jnp.abs(slope)) * (1.0 if a == b else 2.0)

    packs[1].wait_recv()
    packs[3].wait_recv()
    gather((0, 1, 3), near)
    own_pairs(near)
    for i, b in enumerate((2, 3, 6, 7)):
        for a in (2, 3, 6, 7)[:i + 1]:
            other_pairs(a, b)
    packs[2].wait_recv()

    for r in range(1, 4):
        pl.semaphore_signal(ready, inc=1, device_id=neighbour(r), device_id_type=MESH)
    gather(range(SPLIT), far)
    own_pairs(far)
    for b in far:
        for a in (2, 3, 6, 7, 4, 5)[:b + 1]:
            other_pairs(a, b)
    totals = [jnp.sum(x, axis=0, keepdims=True) for x in pushes]
    stack = jnp.concatenate([*pieces(jnp.concatenate(totals, axis=0)), jnp.zeros((8, 128), BF16)], axis=0)
    stack_row = lax.broadcasted_iota(I32, (32, 128), 0)
    query_total = jnp.zeros((32, 256), F32)
    for b in range(TILES):
        query_total += jnp.dot(
            jnp.where(stack_row % 8 == b, stack, jnp.zeros_like(stack)), same[128 * b:128 * b + 128, :],
            preferred_element_type=F32,
        )
    query_total = jnp.sum(query_total, axis=0, keepdims=True)
    factor = jnp.log2(1.0 + query_total) / jnp.maximum(query_total, 1.0)

    stats = []
    for h in range(2):
        own_factor = factor[:, 128 * h:128 * h + 128]
        grad = -jnp.sum(slopes[h], axis=0, keepdims=True) * own_factor
        hess = jnp.sum(curves[h], axis=0, keepdims=True) * own_factor
        out_ref[4 + h:5 + h, 0:128] = grad
        out_ref[6 + h:7 + h, 0:128] = hess
        node = node_ref[h:h + 1, :]
        for value in (grad, hess):
            for n in range(2):
                stats.append(jnp.where(node == n, value, 0.0))
    stat_tx[...] = jnp.concatenate(stats, axis=0)

    def send_stats(peer, far):
        def body(i, carry):
            to = peer(i)
            pltpu.make_async_remote_copy(
                src_ref=stat_tx, dst_ref=stat_rx.at[slot(to[0])], send_sem=stat_send, recv_sem=stat_recv.at[far],
                device_id=device(to), device_id_type=MESH,
            ).start()
            return carry
        return body

    lax.fori_loop(0, PLANE - ROW, send_stats(far_peer, 1), 0)
    lax.fori_loop(0, ROW - 1, send_stats(near_peer, 0), 0)
    stat_rx[inner] = stat_tx[...]
    send_codes(1)

    def prepare(s, carry):
        value = stat_rx[s]
        high = value.astype(BF16).astype(F32)
        low = value - high
        for h in range(2):
            a, b = high[4 * h:4 * h + 4], low[4 * h:4 * h + 4]
            split[s, :, 128 * h:128 * h + 128] = jnp.concatenate([a, b, a, b], axis=0).astype(BF16)
        return carry

    row16 = lax.broadcasted_iota(I32, (16, 128), 0)
    highs = [(row16 // 8 + 2 * i).astype(BF16) for i in range(QUAD // 2)]
    lows = [(row16 + 16 * i).astype(BF16) for i in range(LOW // 16)]
    one, zero = jnp.ones((16, 128), BF16), jnp.zeros((16, 128), BF16)
    start = (sums * 175 * 32) % BINS

    firsts = [(start + 4 * i * OWNED) // BINS for i in range(4)]

    def slot_at(i):
        first, second, late = i, firsts[0] + 3, i - 16
        for k in range(4):
            first = jnp.where(i >= 3 * k, firsts[ORDER[k]] + i - 3 * k, first)
            second = jnp.where(i >= 12 + k, firsts[k] + 3, second)
            late = late + jnp.where(late >= firsts[k], 4, 0)
        return jnp.where(i < 12, first, jnp.where(i < 16, second, late))

    plan = [2, 3, 4, 4, 0, 3, 4, 4, 2, 3, 5, 5, 1, 3, 5, 5]

    def operands(slots, s):
        left, right = [], []
        for slot in slots:
            left_half, right_half = [], []
            for h in range(2):
                code = codes_rx[s, slot, h:h + 1, :]
                low = jnp.broadcast_to(code & (LOW - 1), (16, 128)).astype(BF16)
                high = jnp.broadcast_to(code >> 6, (16, 128)).astype(BF16)
                stat = split[s, :, 128 * h:128 * h + 128]
                left_half.append(jnp.concatenate([jnp.where(low == x, one, zero) for x in lows], axis=0))
                right_half.append(jnp.concatenate([jnp.where(high == x, stat, zero) for x in highs], axis=0))
            left.append(jnp.concatenate(left_half, axis=1))
            right.append(jnp.concatenate(right_half, axis=1))
        return jnp.concatenate(left, axis=0), jnp.concatenate(right, axis=0)

    def product(slots, sources):
        both = [operands(slots, s) for s in sources]
        return lax.dot_general(
            jnp.concatenate([a for a, _ in both], axis=1), jnp.concatenate([b for _, b in both], axis=1),
            (((1,), (1,)), ((), ())), preferred_element_type=F32,
        )

    def slots_of(g):
        return [slot_at(g * QUAD + f) for f in range(QUAD)]

    def near_quad(g, carry):
        tables[g] = product(slots_of(g), range(ROW))
        return carry

    def far_quad(g, carry):
        slots = slots_of(g)
        finish(g, slots, tables[g] + product(slots, range(ROW, PLANE)))
        return carry

    def whole_quad(g, carry):
        slots = slots_of(g)

        @pl.when(g == SLOTS // QUAD - 1)
        def _():
            wait_codes(1, 0, code_recv)
            wait_codes(1, 1, code_recv)

        finish(g, slots, product(slots, range(PLANE)))
        return carry

    def finish(g, slots, table):
        table = table.T
        for f in range(QUAD):
            for high in range(QUAD):
                r = 8 * (QUAD * f + high)
                halves = table[r:r + 8, LOW * f:LOW * f + LOW]
                hist[2 * slots[f] + high // 2, :, LOW * (high % 2):LOW * (high % 2) + LOW] = halves[0:4] + halves[4:8]

        for j in range(DEPTH):
            @pl.when(g == plan[j])
            def _(j=j):
                window = hist.at[pl.ds((start + j * OWNED) // 128, WINDOW)]
                mine = jnp.logical_and(sums == block, j == place)

                @pl.when(mine)
                def _():
                    window_rx[level] = window[...]

                @pl.when(jnp.logical_not(mine))
                def _():
                    pltpu.make_async_remote_copy(
                        src_ref=window, dst_ref=window_rx.at[level],
                        send_sem=final_send.at[j], recv_sem=final_recv.at[level],
                        device_id=(sums * 4 + j // 4, j % 4), device_id_type=MESH,
                    ).start()

    wait_codes(0, 0, code_recv)
    wait_bytes(stat_rx.at[pl.ds(0, ROW - 1)], stat_recv.at[0])
    lax.fori_loop(0, ROW, prepare, 0, unroll=4)
    lax.fori_loop(0, AHEAD, near_quad, 0)
    wait_bytes(stat_rx.at[pl.ds(0, PLANE - ROW)], stat_recv.at[1])
    lax.fori_loop(ROW, PLANE, prepare, 0, unroll=4)
    wait_codes(0, 1, code_recv)
    pl.semaphore_wait(ready, 3)
    lax.fori_loop(0, AHEAD, far_quad, 0)
    lax.fori_loop(AHEAD, SLOTS // QUAD, whole_quad, 0)

    def arrive(k, total):
        @pl.when(jnp.logical_or(sums != block, k != level))
        def _():
            wait_bytes(window_rx.at[k], final_recv.at[k])
        return total + window_rx[k]

    total = lax.fori_loop(0, DEPTH, arrive, jnp.zeros((WINDOW, 4, 128), F32))
    line = jnp.concatenate([total[i] for i in range(WINDOW)], axis=1) * (1.0 / 16.0)
    offset = ((block * 175 * 32) % BINS + place * OWNED) % 128
    out_ref[0:4, :] = pltpu.roll(jnp.concatenate([line, line], axis=0), WINDOW * 128 - offset, 1)[0:4, 0:WIDE]

    for copy in packs.values():
        copy.wait_send()
    for late in range(2):
        for far in range(2):
            wait_codes(late, far, code_send)
    wait_bytes(stat_rx.at[pl.ds(0, PLANE - 1)], stat_send)

    def sent(j, carry):
        @pl.when(jnp.logical_or(sums != block, j != place))
        def _():
            wait_bytes(window_rx.at[j], final_send.at[j])
        return carry

    lax.fori_loop(0, DEPTH, sent, 0)


def unpack(packed_ref, grad_ref, hess_ref, grad_hist_ref, hess_hist_ref):
    grad_ref[...] = packed_ref[4:6, 0:128]
    hess_ref[...] = packed_ref[6:8, 0:128]
    grad_hist_ref[...] = packed_ref[0:2, 0:OWNED]
    hess_hist_ref[...] = packed_ref[2:4, 0:OWNED]


def shards(scores, grades, lengths, bin_codes, node_ids):
    vmem = pl.BlockSpec(memory_space=pltpu.VMEM)
    dma = pltpu.SemaphoreType.DMA
    rows = 2, 128
    packed = pl.pallas_call(
        kernel,
        out_shape=jax.ShapeDtypeStruct((8, WIDE), F32),
        in_specs=[pl.BlockSpec(memory_space=pl.ANY)] * 5,
        out_specs=vmem,
        scratch_shapes=[
            pltpu.VMEM(rows, F32),
            pltpu.VMEM(rows, I32),
            pltpu.VMEM((1, 128), I32),
            pltpu.VMEM((FEATURES, 256), I32),
            pltpu.VMEM(rows, I32),
            pltpu.VMEM((FEATURES + 4, 2, 128), I32),
            pltpu.VMEM((PLANE, SLOTS, 2, 128), I32),
            pltpu.VMEM((2, 2, 128), F32),
            pltpu.VMEM((SPLIT, 2, 2, 128), F32),
            pltpu.VMEM((8, 128), F32),
            pltpu.VMEM((PLANE, 8, 128), F32),
            pltpu.VMEM((PLANE, 16, 256), BF16),
            pltpu.VMEM((8, 128), F32),
            pltpu.VMEM((8, 128), F32),
            pltpu.VMEM((8, 128), F32),
            pltpu.VMEM((8, 128), F32),
            pltpu.VMEM((128 * TILES, 256), F32),
            pltpu.VMEM((128 * TILES, 256), F32),
            pltpu.VMEM((128 * TILES, 256), BF16),
            pltpu.VMEM((AHEAD, QUAD * LOW, QUAD * QUAD * 8), F32),
            pltpu.VMEM((2 * SLOTS, 4, 128), F32),
            pltpu.VMEM((DEPTH, WINDOW, 4, 128), F32),
            dma((5,)),
            dma((SPLIT,)),
            dma((SPLIT,)),
            dma((4,)),
            dma((4,)),
            dma,
            dma((2,)),
            dma((DEPTH,)),
            dma((DEPTH,)),
            pltpu.SemaphoreType.REGULAR,
        ],
        compiler_params=pltpu.CompilerParams(
            collective_id=0, has_side_effects=True, vmem_limit_bytes=60 * 2**20
        ),
        cost_estimate=pl.CostEstimate(flops=10**9, bytes_accessed=10**6, transcendentals=10**6),
    )(scores.reshape(rows), grades.reshape(rows), lengths, bin_codes, node_ids.reshape(rows))
    grad, hess, grad_hist, hess_hist = pl.pallas_call(
        unpack,
        out_shape=[jax.ShapeDtypeStruct(shape, F32) for shape in (rows, rows, (2, OWNED), (2, OWNED))],
        in_specs=[vmem],
        out_specs=[vmem] * 4,
    )(packed)
    return grad.reshape(-1), hess.reshape(-1), grad_hist, hess_hist


def solution(mesh):
    rows = P(("dp", "qsplit"))
    bins = P(None, ("dp", "qsplit"))
    return jax.shard_map(
        shards,
        mesh=mesh,
        in_specs=(rows, rows, P("dp", None), bins, rows),
        out_specs=(rows, rows, bins, bins),
        check_vma=False,
    )
```
